1024 devices in a mesh: group: 64 (over y, x, core), expert: 16 (over z).
Axes of the slice: x: 4, y: 8, z: 16, core: 2. Of those that a mesh axis runs over, the one named last changes fastest.
Arguments:
- tokens: bfloat16 [256, 4, 1792], P('group', None, 'expert'), may hold values from -6 to 6
- out_grad: bfloat16 [256, 4, 1792], P('group', None, 'expert'), may hold values from -6 to 6
- route_weights: bfloat16 [256, 8], P('group'), may hold values from 0.049804688 to 0.5
- expert_ids: int32 [256, 8], P('group'), may hold values from 0 to 15, all different within a row; in each aligned block of 4 rows (0 to 3, 4 to 7, ...) at most 4 rows name the same one
- w_gate: bfloat16 [64, 1792, 2048], P('group', None, 'expert'), may hold values from -0.0625 to 0.0625
- w_up: bfloat16 [64, 1792, 2048], P('group', None, 'expert'), may hold values from -0.0625 to 0.0625
- w_down: bfloat16 [64, 2048, 1792], P('group', 'expert'), may hold values from -0.125 to 0.125
Outputs:
- token_grad: bfloat16 [256, 4, 1792], P('group', None, 'expert')
- down_grad: bfloat16 [64, 2048, 1792], P('group', 'expert')
- route_grad: float32 [256, 8], P('group')
The draws below stay inside these ranges and needn't reach their ends.
Inputs may be any that keep to these rules, and one draw needn't show every extreme that they name: `expert_ids`: each row names 8 different experts; among the 4 rows of one index of group, no expert is named more than 4 times, a bound that some block reaches.
All inputs are finite; a program needn't handle non-finite values.
Results may differ from the reference program's by a relative error of at most 0.029.
Values may be sent and summed in bfloat16 or wider, within the bound.
No kernel may reach another device: no remote copies, remote signals or barrier semaphores. Data moves between devices by JAX's collectives and lax.ppermute only.
A program may use at most 32 MiB of HBM per device.

```python
import math
import jax
import jax.numpy as jnp
import numpy as np
from jax import lax

D = 7168
FF = 2048
OWNERS = 4
TOK_G = 4
EXPERTS_WIN = 16
TOP_K = 8
CAP = 4
TOKENS = 256
N_GROUP = 64
N_EXPERT = 16


def block_levels(rng, extent, cuts, smallest, largest):
    def one(dim, shards_of):
        draws = jax.random.uniform(jax.random.fold_in(jax.random.fold_in(rng, 6), dim), (shards_of,), jnp.float32, smallest / len(cuts), largest / len(cuts))
        return jnp.repeat(jnp.exp(draws), extent[dim] // shards_of).reshape((-1,) + (1,) * (len(extent) - dim - 1))

    loudness = one(*cuts[0])
    for cut in cuts[1:]:
        loudness = loudness * one(*cut)
    return loudness


def deal_out(own_key, own, number, rows, count, top, limit, skew):
    sequence = jax.random.permutation(own_key, count)
    packed, usual = shares(count, rows * top, limit, skew, True), shares(count, rows * top, limit, skew, False)
    places = jnp.arange(count)

    def named(tallies, turn):
        used = int((tallies > 0).sum())
        fixed = max(1, used // 4)
        moved = fixed + (places - fixed + turn * (used - fixed)) % max(1, count - fixed)
        return jnp.zeros((count,), jnp.int32).at[sequence[jnp.where(places < fixed, places, moved)]].set(jnp.asarray(tallies, jnp.int32))

    tallies = jnp.where(number % 4 == 0, named(packed, number // 4), named(usual, number - number // 4 - 1))
    mixed = jax.random.permutation(jax.random.fold_in(own, 3), count)
    donor, receiver = mixed[0:count // 2 * 2:2], mixed[1:count // 2 * 2:2]
    room = jnp.minimum(tallies[donor] - 1, limit - tallies[receiver]) // 2
    room = jnp.where((donor == sequence[0]) | (receiver == sequence[0]) | (tallies[receiver] == 0), 0, jnp.maximum(room, 0))
    moved = jax.random.randint(jax.random.fold_in(own, 4), (count // 2,), 0, 1 << 20) % (room + 1)
    tallies = tallies.at[donor].add(-moved).at[receiver].add(moved)
    members = jnp.searchsorted(jnp.cumsum(tallies), jnp.arange(rows * top), side="right").astype(jnp.int32)
    table = members.reshape(top, rows).T
    table = table[jax.random.permutation(jax.random.fold_in(own, 1), rows)]
    turn = jax.random.randint(jax.random.fold_in(own, 2), (rows, 1), 0, top)
    return jnp.take_along_axis(table, (jnp.arange(top)[None, :] + turn) % top, axis=1)


def shares(count, total, reach, skew, full):
    loads = [(1 << 20) // math.isqrt(grade ** skew) + 1 for grade in range(1, count + 1)]
    largest = reach if full else min(reach, max(-(-total // count), total * loads[0] // sum(loads)))
    least = 1 if total - largest >= count - 1 else 0
    holding, rest = [largest] + [least] * (count - 1), total - largest - least * (count - 1)
    while rest > 0:
        free = [i for i in range(1, count) if holding[i] < largest] or [i for i in range(1, count) if holding[i] < reach]
        whole, budget = sum([loads[i] for i in free]), rest
        for i in free:
            more = min(reach - holding[i], max(1, budget * loads[i] // whole), rest)
            holding[i] = holding[i] + more
            rest = rest - more
    return np.array(holding)


def gaussian(key, extent, spread, reach, cuts=(), kind=jnp.bfloat16):
    result = spread * jax.random.normal(key, extent, jnp.float32)
    if cuts:
        result = result * block_levels(key, extent, cuts, -0.22, 0.18)
    return jnp.clip(result, -reach, reach).astype(kind)


def setup_inputs(seed: int = 0) -> dict:
    seeds = jax.random.split(jax.random.key(seed), 8)
    tokens = gaussian(seeds[0], (TOKENS, OWNERS, D // OWNERS), 1.0, 6.0, ((0, 64), (2, 16)))
    out_grad = gaussian(seeds[1], (TOKENS, OWNERS, D // OWNERS), 1.0, 6.0, ((0, 64), (2, 16)))
    route_weights = jnp.clip(0.049804688 + 0.4501953 * jax.random.uniform(seeds[2], (TOKENS, TOP_K), jnp.float32) ** block_levels(seeds[2], (TOKENS, TOP_K), ((0, 64),), -0.2, 0.2), 0.049804688, 0.5).astype(jnp.bfloat16)
    expert_ids_keys = jax.random.split(jax.random.fold_in(seeds[3], 1), TOKENS // TOK_G)
    expert_ids_turns = jax.random.permutation(jax.random.fold_in(seeds[3], 3), TOKENS // TOK_G)
    expert_ids = jax.vmap(lambda own, number: deal_out(jax.random.fold_in(seeds[3], 2), own, number, TOK_G, EXPERTS_WIN, TOP_K, CAP, 2))(expert_ids_keys, expert_ids_turns).reshape((TOKENS, TOP_K))
    w_gate = gaussian(seeds[4], (EXPERTS_WIN * OWNERS, D // OWNERS, FF), D ** -0.5, 0.0625, ((0, 64), (2, 16)))
    w_up = gaussian(seeds[5], (EXPERTS_WIN * OWNERS, D // OWNERS, FF), D ** -0.5, 0.0625, ((0, 64), (2, 16)))
    w_down = gaussian(seeds[6], (EXPERTS_WIN * OWNERS, FF, D // OWNERS), FF ** -0.5, 0.125, ((0, 64), (1, 16)))
    return {"tokens": tokens, "out_grad": out_grad, "route_weights": route_weights, "expert_ids": expert_ids, "w_gate": w_gate, "w_up": w_up, "w_down": w_down}


def routing_rows(expert_ids):
    onehot = (expert_ids[:, :, None] == jnp.arange(EXPERTS_WIN, dtype=jnp.int32)[None, None, :]).astype(jnp.int32)
    blocks = onehot.reshape(N_GROUP, TOK_G * TOP_K, EXPERTS_WIN)
    slot_pos = jnp.sum((jnp.cumsum(blocks, axis=1) - 1) * blocks, axis=2).reshape(-1)
    source = jnp.arange(TOKENS * TOP_K, dtype=jnp.int32) // (TOK_G * TOP_K)
    experts_flat = expert_ids.reshape(-1).astype(jnp.int32)
    return (experts_flat * (N_GROUP * CAP) + source * CAP + slot_pos).astype(jnp.int32)


def per_expert(items):
    slot_in, slot_grad, slot_weight, gate_w, up_w, down_w = items
    gate_pre = jnp.dot(slot_in, gate_w, preferred_element_type=jnp.float32)
    up_pre = jnp.dot(slot_in, up_w, preferred_element_type=jnp.float32)
    sigmoid_gate = jax.nn.sigmoid(gate_pre)
    hidden = (gate_pre * sigmoid_gate * up_pre).astype(jnp.bfloat16)
    hidden_grad = jnp.dot(slot_grad, down_w.T, preferred_element_type=jnp.float32)
    slot_route = jnp.sum(hidden.astype(jnp.float32) * hidden_grad, axis=1)
    weight_col = slot_weight[:, None]
    weighted_hidden = (weight_col * hidden.astype(jnp.float32)).astype(jnp.bfloat16)
    down_grad = jnp.dot(weighted_hidden.T, slot_grad, preferred_element_type=jnp.float32).astype(jnp.bfloat16)
    scaled = weight_col * hidden_grad
    gate_grad = (scaled * up_pre * sigmoid_gate * (1.0 + gate_pre * (1.0 - sigmoid_gate))).astype(jnp.bfloat16)
    up_grad = (scaled * gate_pre * sigmoid_gate).astype(jnp.bfloat16)
    rows = slot_in.shape[0]
    block_ff = FF // N_EXPERT
    gate_blocks = gate_grad.reshape(rows, N_EXPERT, block_ff).transpose(1, 0, 2)
    up_blocks = up_grad.reshape(rows, N_EXPERT, block_ff).transpose(1, 0, 2)
    gate_wb = gate_w.reshape(D, N_EXPERT, block_ff).transpose(1, 0, 2)
    up_wb = up_w.reshape(D, N_EXPERT, block_ff).transpose(1, 0, 2)

    def add_block(total, pieces):
        gate_piece, up_piece, gate_wpiece, up_wpiece = pieces
        part = jnp.dot(gate_piece, gate_wpiece.T, preferred_element_type=jnp.float32) + jnp.dot(up_piece, up_wpiece.T, preferred_element_type=jnp.float32)
        rounded = lax.optimization_barrier(part.astype(jnp.bfloat16))
        return total + rounded.astype(jnp.float32), None

    slot_input_grad, unused = lax.scan(add_block, jnp.zeros((rows, D), jnp.float32), (gate_blocks, up_blocks, gate_wb, up_wb))
    return slot_input_grad, slot_route, down_grad


def reference(tokens, out_grad, route_weights, expert_ids, w_gate, w_up, w_down):
    rows = N_GROUP * CAP
    owned = routing_rows(expert_ids)
    flat_tokens = tokens.reshape(TOKENS, D)
    flat_grads = out_grad.reshape(TOKENS, D)
    gate_full = w_gate.reshape(EXPERTS_WIN, D, FF)
    up_full = w_up.reshape(EXPERTS_WIN, D, FF)
    down_full = w_down.reshape(EXPERTS_WIN, OWNERS, FF, D // OWNERS).transpose(0, 2, 1, 3).reshape(EXPERTS_WIN, FF, D)
    slot_in = jnp.zeros((EXPERTS_WIN * rows, D), jnp.bfloat16).at[owned].set(jnp.repeat(flat_tokens, TOP_K, axis=0))
    slot_grad = jnp.zeros((EXPERTS_WIN * rows, D), jnp.bfloat16).at[owned].set(jnp.repeat(flat_grads, TOP_K, axis=0))
    slot_weight = jnp.zeros((EXPERTS_WIN * rows,), jnp.float32).at[owned].set(route_weights.reshape(-1).astype(jnp.float32))
    slot_input_grad, slot_route, down_grad = lax.map(per_expert, (slot_in.reshape(EXPERTS_WIN, rows, D), slot_grad.reshape(EXPERTS_WIN, rows, D), slot_weight.reshape(EXPERTS_WIN, rows), gate_full, up_full, down_full))
    per_route = slot_input_grad.reshape(EXPERTS_WIN * rows, D)[owned].reshape(TOKENS, TOP_K, D)
    token_grad = jnp.sum(per_route, axis=1).astype(jnp.bfloat16).reshape(TOKENS, OWNERS, D // OWNERS)
    route_grad = slot_route.reshape(-1)[owned].reshape(TOKENS, TOP_K)
    down_out = down_grad.reshape(EXPERTS_WIN, FF, OWNERS, D // OWNERS).transpose(0, 2, 1, 3).reshape(EXPERTS_WIN * OWNERS, FF, D // OWNERS)
    return token_grad, down_out, route_grad
```

```python
import jax
import jax.numpy as jnp
from jax import lax
from jax.sharding import Mesh, PartitionSpec as P

OWNERS = 4
LANES = 128


def split_hi_lo(v):
    hi = v.astype(jnp.bfloat16)
    lo = (v - hi.astype(jnp.float32)).astype(jnp.bfloat16)
    return hi, lo


def weight_table(expert_ids, route_weights, experts):
    onehot = expert_ids[:, :, None] == jnp.arange(experts, dtype=jnp.int32)[None, None, :]
    weights = jnp.where(onehot, route_weights.astype(jnp.float32)[:, :, None], 0.0)
    return jnp.sum(weights, axis=1).astype(jnp.bfloat16), onehot


def y_ring(block):
    count = lax.axis_size("y")
    up = [(i, (i + 1) % count) for i in range(count)]
    down = [((i + 1) % count, i) for i in range(count)]
    blocks = [None] * count
    blocks[0] = block
    fwd = bwd = block
    for step in range(1, count // 2 + 1):
        fwd = lax.ppermute(fwd, "y", up)
        blocks[(-step) % count] = fwd
        if step < count // 2:
            bwd = lax.ppermute(bwd, "y", down)
            blocks[step] = bwd
    return blocks


def body(tokens, out_grad, route_weights, expert_ids, w_gate, w_up, w_down):
    f32, bf16 = jnp.float32, jnp.bfloat16
    ny, nxh, nz = lax.axis_size("y"), lax.axis_size("xh"), lax.axis_size("z")
    experts = ny * nxh
    toks, _, sub = tokens.shape
    per_y = nxh * OWNERS
    groups = ny * per_y
    my_y = lax.axis_index("y")
    expert = my_y * nxh + lax.axis_index("xh")

    table, onehot = weight_table(expert_ids, route_weights, experts)
    x_rows = jnp.concatenate(
        [tokens.transpose(1, 0, 2), jnp.broadcast_to(table[None], (OWNERS, toks, experts))], axis=2
    )
    g_rows = jnp.pad(out_grad.transpose(1, 0, 2), ((0, 0), (0, 0), (0, LANES - sub)))
    send = jnp.concatenate([x_rows, g_rows], axis=1)
    send = jnp.broadcast_to(
        send[None, :, None], (nxh, OWNERS, nz, 2 * toks, LANES)
    ).reshape(nxh * OWNERS * nz, 2 * toks, LANES)
    got = lax.all_to_all(send, ("xh", "xl", "c", "z"), 0, 0, tiled=True)

    blocks = y_ring(got)

    gate_p = jnp.pad(w_gate[0].reshape(nz, sub, LANES), ((0, 0), (0, LANES - sub), (0, 0)))
    up_p = jnp.pad(w_up[0].reshape(nz, sub, LANES), ((0, 0), (0, LANES - sub), (0, 0)))
    gate_up = jnp.concatenate([gate_p, up_p], axis=2).reshape(nz * LANES, 2 * LANES)
    down_p = jnp.pad(w_down[0].reshape(LANES, nz, sub), ((0, 0), (0, 0), (0, LANES - sub)))
    down_p = down_p.reshape(LANES, nz * LANES)

    mats, parts = [], []
    for block in blocks:
        mat = (
            block.reshape(per_y, nz, 2 * toks, LANES)
            .transpose(0, 2, 1, 3)
            .reshape(per_y * 2 * toks, nz * LANES)
        )
        first = jnp.dot(mat, gate_up, preferred_element_type=f32)
        second = lax.dot_general(mat, down_p, (((1,), (1,)), ((), ())), preferred_element_type=f32)
        first = first.reshape(per_y, 2 * toks, 2 * LANES)[:, :toks]
        second = second.reshape(per_y, 2 * toks, LANES)[:, toks:]
        part = jnp.concatenate([first, second], axis=2).astype(bf16)
        mats.append(mat)
        parts.append(part.reshape(per_y * toks, 3 * LANES))
    rows = jnp.concatenate(mats, axis=0)
    part = jnp.concatenate(parts, axis=0)

    quad = lax.all_gather(part, ("xl", "c"), axis=0, tiled=False)
    sums = jnp.sum(quad.astype(f32), axis=0)
    gate_pre = sums[:, :LANES]
    up_pre = sums[:, LANES : 2 * LANES]
    hidden_grad = sums[:, 2 * LANES :]

    w_rows = rows[:, sub:LANES].reshape(ny * per_y, 2 * toks, experts)[:, :toks]
    mine = jnp.arange(experts, dtype=jnp.int32) == expert
    weight = jnp.sum(jnp.where(mine, w_rows.astype(f32), 0.0), axis=2).reshape(-1, 1)

    sig = jax.nn.sigmoid(gate_pre)
    hidden = (gate_pre * sig * up_pre).astype(bf16)
    route = jnp.sum(hidden.astype(f32) * hidden_grad, axis=1)
    scaled = weight * hidden_grad
    gate_grad = (scaled * up_pre * sig * (1.0 + gate_pre * (1.0 - sig))).astype(bf16)
    up_grad = (scaled * gate_pre * sig).astype(bf16)
    weighted = (weight * hidden.astype(f32)).astype(bf16)

    route_hi, route_lo = split_hi_lo(route)
    extra = jnp.stack([route_hi, route_lo], axis=1)
    small = jnp.concatenate([gate_grad, up_grad, jnp.pad(extra, ((0, 0), (0, LANES - 2)))], axis=1)
    small = small.reshape(ny, per_y * toks, 3 * LANES)
    small = lax.dynamic_slice_in_dim(
        jnp.concatenate([small, small], axis=0), lax.rem(ny - my_y, ny), ny, axis=0
    )
    small = small.reshape(groups, 1, toks, 3 * LANES)
    grads = small[..., : 2 * LANES]
    half = jnp.arange(2)
    lhs = jnp.where(
        (half[:, None] == half[None, :])[None, :, None, :, None],
        grads[:, :, :, None, :],
        jnp.zeros((), bf16),
    )
    lhs = jnp.broadcast_to(lhs, (groups, 2, toks, 2, 2 * LANES)).reshape(
        groups * 2 * toks, 4 * LANES
    )
    halves = gate_up.reshape(2, nz * LANES // 2, 2 * LANES).transpose(0, 2, 1)
    halves = halves.reshape(4 * LANES, nz * LANES // 2)
    back = jnp.dot(lhs, halves, preferred_element_type=f32)
    lane = jnp.arange(nz * LANES // 2, dtype=jnp.int32)
    hi_col = jnp.broadcast_to(
        small[..., 2 * LANES : 2 * LANES + 1], (groups, 2, toks, 1)
    ).reshape(-1, 1)
    lo_col = jnp.broadcast_to(
        small[..., 2 * LANES + 1 : 2 * LANES + 2], (groups, 2, toks, 1)
    ).reshape(-1, 1)
    back = jnp.where(
        lane == sub, hi_col.astype(f32), jnp.where(lane == sub + 1, lo_col.astype(f32), back)
    )
    back = back.astype(bf16).reshape(groups, 2 * toks, nz * LANES // 2)
    landed = lax.all_to_all(back, ("y", "xh", "xl", "c"), 0, 0, tiled=True)

    wide = jnp.pad(
        weighted.reshape(groups, toks, LANES), ((0, 0), (0, toks), (0, 0)), constant_values=0
    )
    g_only = jnp.concatenate([wide[:, toks:], wide[:, :toks]], axis=1).reshape(-1, LANES)
    down_grad = lax.dot_general(
        g_only, rows, (((0,), (0,)), ((), ())), preferred_element_type=f32
    ).astype(bf16)
    down_grad = down_grad.reshape(LANES, nz, LANES)[:, :, :sub].reshape(1, LANES, nz * sub)

    landed = landed.reshape(experts, OWNERS, 2 * toks, nz * LANES // 2).astype(f32)
    summed = jnp.sum(landed, axis=0)
    route_part = landed[:, 0, :toks, sub] + landed[:, 0, :toks, sub + 1]
    part_hi, part_lo = split_hi_lo(route_part.T)
    zero = jnp.zeros_like(part_hi)
    pad_rows = jnp.concatenate([part_hi, part_lo, zero, zero], axis=0)
    pieces = (
        summed.astype(bf16)
        .reshape(OWNERS, 2, toks, nz // 2, LANES)
        .transpose(1, 3, 0, 2, 4)
        .reshape(nz, OWNERS * toks, LANES)
    )
    pieces = jnp.concatenate(
        [pieces[..., :sub], jnp.broadcast_to(pad_rows[None], (nz, OWNERS * toks, experts))], axis=2
    )
    final = lax.all_to_all(pieces, "z", 0, 0, tiled=True)
    final = jnp.sum(final.astype(f32), axis=0)
    token_grad = final[:, :sub].reshape(OWNERS, toks, sub).transpose(1, 0, 2).astype(bf16)
    routes = final[:toks, sub:] + final[toks : 2 * toks, sub:]
    route_grad = jnp.sum(jnp.where(onehot, routes[:, None, :], 0.0), axis=2)
    return token_grad, down_grad, route_grad


def solution(mesh):
    fine = Mesh(
        mesh.devices.reshape(-1, 2, 2, 2, mesh.devices.shape[1]), ("y", "xh", "xl", "c", "z")
    )
    group = ("y", "xh", "xl", "c")
    return jax.shard_map(
        body,
        mesh=fine,
        in_specs=(
            P(group, None, "z"),
            P(group, None, "z"),
            P(group, None),
            P(group, None),
            P(group, None, "z"),
            P(group, None, "z"),
            P(group, "z", None),
        ),
        out_specs=(P(group, None, "z"), P(group, "z", None), P(group, None)),
        check_vma=False,
    )
```

```python
import functools

import jax
import jax.numpy as jnp
from jax import lax
from jax.experimental import pallas as pl
from jax.experimental.pallas import tpu as pltpu
from jax.sharding import Mesh, PartitionSpec as P

OWNERS = 4
LANES = 128


VMEM_LIMIT = 40 * 1024 * 1024


def hi_lo(v):
    hi = v.astype(jnp.bfloat16).astype(jnp.float32)
    return hi, v - hi


def call(kernel, out_shape, in_specs, scratch, flops, moved):
    return pl.pallas_call(
        kernel,
        out_shape=out_shape,
        in_specs=in_specs,
        out_specs=jax.tree.map(lambda _: pl.BlockSpec(memory_space=pltpu.VMEM), out_shape),
        scratch_shapes=scratch,
        compiler_params=pltpu.CompilerParams(vmem_limit_bytes=VMEM_LIMIT),
        cost_estimate=pl.CostEstimate(flops=flops, bytes_accessed=moved, transcendentals=0),
    )


def whole(count):
    return [pl.BlockSpec(memory_space=pltpu.VMEM)] * count


def upper(shape):
    return lax.broadcasted_iota(jnp.int32, shape, len(shape) - 2) >= 4


def swap(v):
    return pltpu.roll(v, 4, axis=v.ndim - 2)


def first_fours(v):
    pairs = v.reshape(v.shape[0] // 16, 2, 8, v.shape[1])
    even, odd = pairs[:, 0], pairs[:, 1]
    return jnp.where(upper(even.shape), swap(odd), even).reshape(-1, v.shape[1])


def last_fours(v):
    pairs = v.reshape(v.shape[0] // 16, 2, 8, v.shape[1])
    even, odd = pairs[:, 0], pairs[:, 1]
    return jnp.where(upper(even.shape), odd, swap(even)).reshape(-1, v.shape[1])


def lay_rows(my_y, blocks, rows):
    count = len(blocks)
    for index, block in enumerate(blocks):
        per_y, nz, tall, _ = block.shape
        size = per_y * tall
        base = pl.multiple_of(lax.rem(my_y + index, count) * size, size)
        for z in range(nz):
            tile = block[:, z].astype(jnp.float32).reshape(size, LANES).astype(jnp.bfloat16)
            rows[pl.ds(base, size), z * LANES : (z + 1) * LANES] = tile


def part_kernel(place, *refs):
    *blocks, gate_up, down, part, weight, rows = refs
    f32 = jnp.float32
    lay_rows(place[0], blocks, rows)
    mat = rows[...]
    first = jnp.dot(mat, gate_up[...], preferred_element_type=f32)
    second = lax.dot_general(mat, down[...], (((1,), (1,)), ((), ())), preferred_element_type=f32)
    part[:, : 2 * LANES] = first_fours(first).astype(part.dtype)
    part[:, 2 * LANES :] = last_fours(second).astype(part.dtype)
    tags = rows[:, :LANES].astype(f32)
    lane = lax.broadcasted_iota(jnp.int32, tags.shape, 1)
    tags = jnp.sum(jnp.where(lane == place[1], tags, 0.0), axis=1, keepdims=True)
    weight[...] = first_fours(jnp.broadcast_to(tags, mat[:, :LANES].shape))


def grad_kernel(sub, quad, weight, halves, back, wide):
    f32, bf16 = jnp.float32, jnp.bfloat16
    sums = quad[0].astype(f32)
    for index in range(1, OWNERS):
        sums = sums + quad[index].astype(f32)
    gate_pre = sums[:, :LANES]
    up_pre = sums[:, LANES : 2 * LANES]
    hidden_grad = sums[:, 2 * LANES :]
    sig = jax.nn.sigmoid(gate_pre)
    hidden = (gate_pre * sig * up_pre).astype(bf16).astype(f32)
    route = jnp.sum(hidden * hidden_grad, axis=1, keepdims=True)
    scaled = weight[...] * hidden_grad
    gate_grad = (scaled * up_pre * sig * (1.0 + gate_pre * (1.0 - sig))).astype(bf16)
    up_grad = (scaled * gate_pre * sig).astype(bf16)
    both = jnp.concatenate([gate_grad, up_grad], axis=1)
    route_hi, route_lo = hi_lo(route)
    pairs = both.shape[0] // 8
    width = halves.shape[2]
    step = 2 * LANES
    for start in range(0, width, step):
        outs = []
        for half in range(2):
            out = jnp.dot(
                both, halves[half, :, start : start + step], preferred_element_type=f32
            )
            if start == 0:
                lane = lax.broadcasted_iota(jnp.int32, out.shape, 1)
                out = jnp.where(lane == sub, route_hi, jnp.where(lane == sub + 1, route_lo, out))
            outs.append(out.reshape(pairs, 8, step))
        top, low = outs
        mask = upper(top.shape)
        even = jnp.where(mask, swap(low), top)
        odd = jnp.where(mask, low, swap(top))
        both_rows = jnp.stack([even, odd], axis=1).reshape(2 * pairs, 8, step)
        back[:, :, start : start + step] = both_rows.astype(bf16)
    weighted = (weight[...] * hidden).reshape(pairs, 8, LANES)
    mask = upper(weighted.shape)
    even = jnp.where(mask, swap(weighted), 0.0)
    odd = jnp.where(mask, weighted, 0.0)
    wide[...] = jnp.stack([even, odd], axis=1).reshape(pairs * 16, LANES).astype(bf16)


def down_kernel(place, *refs):
    *blocks, wide, out, rows = refs
    lay_rows(place[0], blocks, rows)
    out[...] = lax.dot_general(
        wide[...], rows[...], (((0,), (0,)), ((), ())), preferred_element_type=jnp.float32
    ).astype(out.dtype)


def sum_kernel(sub, landed, pieces):
    f32 = jnp.float32
    experts = landed.shape[0]
    width = landed.shape[3]
    tags = jnp.zeros((8, LANES), f32)
    lane = lax.broadcasted_iota(jnp.int32, (8, LANES), 1)
    for e in range(experts):
        pair = landed[e, 0, :, :LANES].astype(f32)
        both = jnp.sum(
            jnp.where((lane == sub) | (lane == sub + 1), pair, 0.0), axis=1, keepdims=True
        )
        tags = jnp.where(lane == sub + e, both, tags)
    tag_hi, tag_lo = hi_lo(tags)
    mask = upper((8, LANES))
    tags = jnp.where(mask, swap(tag_lo), tag_hi)
    for mm in range(width // LANES):
        cols = slice(mm * LANES, (mm + 1) * LANES)
        acc = landed[0, :, :, cols].astype(f32)
        for e in range(1, experts):
            acc = acc + landed[e, :, :, cols].astype(f32)
        for half in range(2):
            tiles = []
            for pair in range(2):
                one, two = acc[2 * pair], acc[2 * pair + 1]
                tile = jnp.where(mask, swap(two), one) if half == 0 else jnp.where(mask, two, swap(one))
                tiles.append(jnp.where(lane < sub, tile, tags if pair == 0 else 0.0))
            full = jnp.concatenate(tiles, axis=0).astype(pieces.dtype)
            pieces[half * (width // LANES) + mm] = full


def weight_table(expert_ids, route_weights, experts):
    onehot = expert_ids[:, :, None] == jnp.arange(experts, dtype=jnp.int32)[None, None, :]
    weights = jnp.where(onehot, route_weights.astype(jnp.float32)[:, :, None], 0.0)
    return jnp.sum(weights, axis=1).astype(jnp.bfloat16), onehot


def y_ring(block):
    count = lax.axis_size("y")
    up = [(i, (i + 1) % count) for i in range(count)]
    down = [((i + 1) % count, i) for i in range(count)]
    blocks = [None] * count
    blocks[0] = block
    fwd = bwd = block
    for step in range(1, count // 2 + 1):
        fwd = lax.ppermute(fwd, "y", up)
        blocks[(-step) % count] = fwd
        if step < count // 2:
            bwd = lax.ppermute(bwd, "y", down)
            blocks[step] = bwd
    return blocks


def body(tokens, out_grad, route_weights, expert_ids, w_gate, w_up, w_down):
    f32, bf16 = jnp.float32, jnp.bfloat16
    ny, nxh, nz = lax.axis_size("y"), lax.axis_size("xh"), lax.axis_size("z")
    experts = ny * nxh
    toks, _, sub = tokens.shape
    per_y = nxh * OWNERS
    groups = ny * per_y
    tall = 2 * toks
    my_y = lax.axis_index("y")
    expert = my_y * nxh + lax.axis_index("xh")
    place = jnp.stack([my_y, sub + expert]).astype(jnp.int32)

    table, onehot = weight_table(expert_ids, route_weights, experts)
    x_rows = jnp.concatenate(
        [tokens.transpose(1, 0, 2), jnp.broadcast_to(table[None], (OWNERS, toks, experts))], axis=2
    )
    g_rows = jnp.pad(out_grad.transpose(1, 0, 2), ((0, 0), (0, 0), (0, LANES - sub)))
    send = jnp.concatenate([x_rows, g_rows], axis=1)
    send = jnp.broadcast_to(send[None, :, None], (nxh, OWNERS, nz, tall, LANES))
    send = send.reshape(nxh * OWNERS * nz, tall, LANES)
    got = lax.all_to_all(send, ("xh", "xl", "c", "z"), 0, 0, tiled=True)
    blocks = [b.reshape(per_y, nz, tall, LANES) for b in y_ring(got)]

    gate_p = jnp.pad(w_gate[0].reshape(nz, sub, LANES), ((0, 0), (0, LANES - sub), (0, 0)))
    up_p = jnp.pad(w_up[0].reshape(nz, sub, LANES), ((0, 0), (0, LANES - sub), (0, 0)))
    gate_up = jnp.concatenate([gate_p, up_p], axis=2).reshape(nz * LANES, 2 * LANES)
    halves = gate_up.reshape(2, nz * LANES // 2, 2 * LANES).transpose(0, 2, 1)
    down_p = jnp.pad(w_down[0].reshape(LANES, nz, sub), ((0, 0), (0, 0), (0, LANES - sub)))
    down_p = down_p.reshape(LANES, nz * LANES)

    smem = pl.BlockSpec(memory_space=pltpu.SMEM)
    slots = groups * toks
    scratch = [pltpu.VMEM((groups * tall, nz * LANES), bf16)]
    part, weight = call(
        part_kernel,
        (
            jax.ShapeDtypeStruct((slots, 3 * LANES), bf16),
            jax.ShapeDtypeStruct((slots, LANES), f32),
        ),
        [smem] + whole(ny + 2),
        scratch,
        2 * groups * tall * nz * LANES * 3 * LANES,
        4 << 20,
    )(place, *blocks, gate_up, down_p)

    quad = lax.all_gather(part, ("xl", "c"), axis=0, tiled=False)

    back, wide = call(
        functools.partial(grad_kernel, sub),
        (
            jax.ShapeDtypeStruct((groups, tall, nz * LANES // 2), bf16),
            jax.ShapeDtypeStruct((groups * tall, LANES), bf16),
        ),
        whole(3),
        [],
        2 * slots * 2 * LANES * nz * LANES,
        3 << 20,
    )(quad, weight, halves)
    landed = lax.all_to_all(back, ("y", "xh", "xl", "c"), 0, 0, tiled=True)

    down_grad = call(
        down_kernel,
        jax.ShapeDtypeStruct((LANES, nz * LANES), bf16),
        [smem] + whole(ny + 1),
        scratch,
        2 * groups * tall * nz * LANES * LANES,
        4 << 20,
    )(place, *blocks, wide)
    down_grad = down_grad.reshape(LANES, nz, LANES)[:, :, :sub].reshape(1, LANES, nz * sub)

    pieces = call(
        functools.partial(sum_kernel, sub),
        jax.ShapeDtypeStruct((nz, OWNERS * toks, LANES), bf16),
        whole(1),
        [],
        groups * tall * nz * LANES // 2,
        1 << 20,
    )(landed.reshape(experts, OWNERS, tall, nz * LANES // 2))
    final = lax.all_to_all(pieces, "z", 0, 0, tiled=True)
    final = jnp.sum(final.astype(f32), axis=0)
    token_grad = final[:, :sub].reshape(OWNERS, toks, sub).transpose(1, 0, 2).astype(bf16)
    routes = final[:toks, sub:] + final[toks : 2 * toks, sub:]
    route_grad = jnp.sum(jnp.where(onehot, routes[:, None, :], 0.0), axis=2)
    return token_grad, down_grad, route_grad


def solution(mesh):
    fine = Mesh(
        mesh.devices.reshape(-1, 2, 2, 2, mesh.devices.shape[1]), ("y", "xh", "xl", "c", "z")
    )
    group = ("y", "xh", "xl", "c")
    return jax.shard_map(
        body,
        mesh=fine,
        in_specs=(
            P(group, None, "z"),
            P(group, None, "z"),
            P(group, None),
            P(group, None),
            P(group, None, "z"),
            P(group, None, "z"),
            P(group, "z", None),
        ),
        out_specs=(P(group, None, "z"), P(group, "z", None), P(group, None)),
        check_vma=False,
    )
```

```python
import functools

import jax
import jax.numpy as jnp
from jax import lax
from jax.experimental import pallas as pl
from jax.experimental.pallas import tpu as pltpu
from jax.sharding import Mesh, PartitionSpec as P

OWNERS = 4
LANES = 128


VMEM_LIMIT = 40 * 1024 * 1024


def hi_lo(v):
    hi = v.astype(jnp.bfloat16).astype(jnp.float32)
    return hi, v - hi


def call(kernel, out_shape, in_specs, scratch, flops, moved):
    return pl.pallas_call(
        kernel,
        out_shape=out_shape,
        in_specs=in_specs,
        out_specs=jax.tree.map(lambda _: pl.BlockSpec(memory_space=pltpu.VMEM), out_shape),
        scratch_shapes=scratch,
        compiler_params=pltpu.CompilerParams(vmem_limit_bytes=VMEM_LIMIT),
        cost_estimate=pl.CostEstimate(flops=flops, bytes_accessed=moved, transcendentals=0),
    )


def whole(count):
    return [pl.BlockSpec(memory_space=pltpu.VMEM)] * count


def upper(shape):
    return lax.broadcasted_iota(jnp.int32, shape, len(shape) - 2) >= 4


def swap(v):
    return pltpu.roll(v, 4, axis=v.ndim - 2)


def first_fours(v):
    pairs = v.reshape(v.shape[0] // 16, 2, 8, v.shape[1])
    even, odd = pairs[:, 0], pairs[:, 1]
    return jnp.where(upper(even.shape), swap(odd), even).reshape(-1, v.shape[1])


def last_fours(v):
    pairs = v.reshape(v.shape[0] // 16, 2, 8, v.shape[1])
    even, odd = pairs[:, 0], pairs[:, 1]
    return jnp.where(upper(even.shape), odd, swap(even)).reshape(-1, v.shape[1])


def lay_rows(my_y, blocks, rows):
    count = len(blocks)
    tiles = rows.shape[1] // LANES
    for index, block in enumerate(blocks):
        per_y = block.shape[0] // tiles
        size = per_y * 8
        base = pl.multiple_of(lax.rem(my_y + index, count) * size, size)
        for k in range(tiles):
            tile = block[k * per_y : (k + 1) * per_y].astype(jnp.float32)
            rows[pl.ds(base, size), k * LANES : (k + 1) * LANES] = tile.reshape(
                size, LANES
            ).astype(jnp.bfloat16)


def pack_kernel(sub, got, block):
    f32 = jnp.float32
    per_y, nz, _, _ = got.shape
    size = per_y * 8
    tiles = nz * sub // LANES
    lane = lax.broadcasted_iota(jnp.int32, (size, LANES), 1)
    for k in range(tiles):
        first, skip = divmod(k * LANES, sub)
        tile = got[:, first].astype(f32).reshape(size, LANES)
        if skip:
            tile = pltpu.roll(tile, LANES - skip, axis=1)
        after = got[:, first + 1].astype(f32).reshape(size, LANES)
        after = pltpu.roll(after, sub - skip, axis=1)
        tile = jnp.where(lane < sub - skip, tile, after)
        block[k * per_y : (k + 1) * per_y] = tile.reshape(per_y, 8, LANES).astype(block.dtype)
    width = LANES - sub
    lane = lax.broadcasted_iota(jnp.int32, (8, LANES), 1)
    tags = jnp.zeros((8, LANES), f32)
    for s in range(per_y):
        moved = pltpu.roll(got[s, 0].astype(f32), (width * s - sub) % LANES, axis=1)
        tags = jnp.where((lane >= width * s) & (lane < width * (s + 1)), moved, tags)
    block[tiles * per_y] = tags.astype(block.dtype)


def part_kernel(place, *refs):
    *blocks, gate, up, down, part, weight, rows, spread = refs
    f32 = jnp.float32
    lay_rows(place[0], blocks, rows)
    mat = rows[...]
    count = len(blocks)
    size = rows.shape[0] // count
    per_y = size // 8
    shape = (per_y, 8, LANES)
    lane = lax.broadcasted_iota(jnp.int32, shape, 2)
    want = place[1] + lax.broadcasted_iota(jnp.int32, shape, 0) * (LANES // per_y)
    for index, block in enumerate(blocks):
        tags = jnp.broadcast_to(block[block.shape[0] - 1].astype(f32)[None], shape)
        tags = jnp.sum(jnp.where(lane == want, tags, 0.0), axis=2, keepdims=True)
        base = pl.multiple_of(lax.rem(place[0] + index, count) * size, size)
        spread[pl.ds(base, size), :] = jnp.broadcast_to(tags, shape).reshape(size, LANES)
    weight[...] = first_fours(spread[...])
    for index, mats in enumerate((gate, up)):
        out = jnp.dot(mat, mats[...], preferred_element_type=f32)
        part[:, index * LANES : (index + 1) * LANES] = first_fours(out).astype(part.dtype)
    out = lax.dot_general(mat, down[...], (((1,), (1,)), ((), ())), preferred_element_type=f32)
    part[:, 2 * LANES :] = last_fours(out).astype(part.dtype)


def grad_kernel(quad, weight, gate, up, back, wide):
    f32, bf16 = jnp.float32, jnp.bfloat16
    sums = quad[0].astype(f32)
    for index in range(1, OWNERS):
        sums = sums + quad[index].astype(f32)
    gate_pre = sums[:, :LANES]
    up_pre = sums[:, LANES : 2 * LANES]
    hidden_grad = sums[:, 2 * LANES :]
    sig = jax.nn.sigmoid(gate_pre)
    hidden = (gate_pre * sig * up_pre).astype(bf16).astype(f32)
    route = jnp.sum(hidden * hidden_grad, axis=1, keepdims=True)
    scaled = weight[...] * hidden_grad
    gate_grad = (scaled * up_pre * sig * (1.0 + gate_pre * (1.0 - sig))).astype(bf16)
    up_grad = (scaled * gate_pre * sig).astype(bf16)
    route_hi, route_lo = hi_lo(route)
    slots = route.shape[0]
    groups, tiles, toks, _ = back.shape
    lane = lax.broadcasted_iota(jnp.int32, (slots, LANES), 1)
    tags = jnp.where(lane == 0, route_hi, jnp.where(lane == 1, route_lo, 0.0))
    back[:, tiles - 1] = tags.reshape(groups, toks, LANES).astype(bf16)
    across = (((1,), (1,)), ((), ()))
    for k in range(0, tiles - 1, 2):
        cols = slice(k * LANES, (k + 2) * LANES)
        out = lax.dot_general(gate_grad, gate[cols], across, preferred_element_type=f32)
        out = out + lax.dot_general(up_grad, up[cols], across, preferred_element_type=f32)
        for j in range(2):
            tile = out[:, j * LANES : (j + 1) * LANES]
            back[:, k + j] = tile.reshape(groups, toks, LANES).astype(bf16)
    pairs = slots // 8
    weighted = (weight[...] * hidden).reshape(pairs, 8, LANES)
    mask = upper(weighted.shape)
    even = jnp.where(mask, swap(weighted), 0.0)
    odd = jnp.where(mask, weighted, 0.0)
    wide[...] = jnp.stack([even, odd], axis=1).reshape(pairs * 16, LANES).astype(bf16)


def down_kernel(place, *refs):
    *blocks, wide, out, rows = refs
    lay_rows(place[0], blocks, rows)
    out[...] = lax.dot_general(
        wide[...], rows[...], (((0,), (0,)), ((), ())), preferred_element_type=jnp.float32
    ).astype(out.dtype)


def sum_kernel(sub, landed, pieces, acc):
    f32 = jnp.float32
    experts, owners, tiles, toks, _ = landed.shape
    tags = jnp.zeros((2 * toks, LANES), f32)
    lane = lax.broadcasted_iota(jnp.int32, (toks, LANES), 1)
    tag_hi = jnp.zeros((toks, LANES), f32)
    for e in range(experts):
        pair = landed[e, 0, tiles - 1].astype(f32)
        both = jnp.sum(jnp.where(lane < 2, pair, 0.0), axis=1, keepdims=True)
        tag_hi = jnp.where(lane == sub + e, both, tag_hi)
    tag_hi, tag_lo = hi_lo(tag_hi)
    acc[tiles - 1] = jnp.zeros_like(acc[tiles - 1])
    acc[tiles - 1, :toks] = tag_hi
    acc[tiles - 1, toks : 2 * toks] = tag_lo
    for k in range(tiles - 1):
        for q in range(owners):
            acc[k, q * toks : (q + 1) * toks] = jnp.sum(landed[:, q, k].astype(f32), axis=0)
    tags = acc[tiles - 1]
    lane = lax.broadcasted_iota(jnp.int32, tags.shape, 1)
    for m in range(pieces.shape[0]):
        first, skip = divmod(m * sub, LANES)
        tile = acc[first]
        if skip:
            tile = pltpu.roll(tile, LANES - skip, axis=1)
        if skip + sub > LANES:
            after = pltpu.roll(acc[first + 1], LANES - skip, axis=1)
            tile = jnp.where(lane < LANES - skip, tile, after)
        pieces[m] = jnp.where(lane < sub, tile, tags).astype(pieces.dtype)


def weight_table(expert_ids, route_weights, experts):
    onehot = expert_ids[:, :, None] == jnp.arange(experts, dtype=jnp.int32)[None, None, :]
    weights = jnp.where(onehot, route_weights.astype(jnp.float32)[:, :, None], 0.0)
    return jnp.sum(weights, axis=1).astype(jnp.bfloat16), onehot


def y_ring(block):
    count = lax.axis_size("y")
    up = [(i, (i + 1) % count) for i in range(count)]
    down = [((i + 1) % count, i) for i in range(count)]
    blocks = [None] * count
    blocks[0] = block
    fwd = bwd = block
    for step in range(1, count // 2 + 1):
        fwd = lax.ppermute(fwd, "y", up)
        blocks[(-step) % count] = fwd
        if step < count // 2:
            bwd = lax.ppermute(bwd, "y", down)
            blocks[step] = bwd
    return blocks


def body(tokens, out_grad, route_weights, expert_ids, w_gate, w_up, w_down):
    f32, bf16 = jnp.float32, jnp.bfloat16
    ny, nxh, nz = lax.axis_size("y"), lax.axis_size("xh"), lax.axis_size("z")
    experts = ny * nxh
    toks, _, sub = tokens.shape
    per_y = nxh * OWNERS
    groups = ny * per_y
    tall = 2 * toks
    my_y = lax.axis_index("y")
    expert = my_y * nxh + lax.axis_index("xh")
    place = jnp.stack([my_y, expert]).astype(jnp.int32)

    table, onehot = weight_table(expert_ids, route_weights, experts)
    x_rows = jnp.concatenate(
        [tokens.transpose(1, 0, 2), jnp.broadcast_to(table[None], (OWNERS, toks, experts))], axis=2
    )
    g_rows = jnp.pad(out_grad.transpose(1, 0, 2), ((0, 0), (0, 0), (0, LANES - sub)))
    send = jnp.concatenate([x_rows, g_rows], axis=1)
    send = jnp.broadcast_to(send[None, :, None], (nxh, OWNERS, nz, tall, LANES))
    send = send.reshape(nxh * OWNERS * nz, tall, LANES)
    got = lax.all_to_all(send, ("xh", "xl", "c", "z"), 0, 0, tiled=True)
    tiles = nz * sub // LANES
    block = call(
        functools.partial(pack_kernel, sub),
        jax.ShapeDtypeStruct((tiles * per_y + 1, tall, LANES), bf16),
        whole(1),
        [],
        groups * tall * LANES,
        1 << 19,
    )(got.reshape(per_y, nz, tall, LANES))
    blocks = y_ring(block)

    smem = pl.BlockSpec(memory_space=pltpu.SMEM)
    slots = groups * toks
    rows = pltpu.VMEM((groups * tall, nz * sub), bf16)
    part, weight = call(
        part_kernel,
        (
            jax.ShapeDtypeStruct((slots, 3 * LANES), bf16),
            jax.ShapeDtypeStruct((slots, LANES), f32),
        ),
        [smem] + whole(ny + 3),
        [rows, pltpu.VMEM((groups * tall, LANES), f32)],
        2 * groups * tall * nz * LANES * 3 * LANES,
        4 << 20,
    )(place, *blocks, w_gate[0], w_up[0], w_down[0])

    quad = lax.all_gather(part, ("xl", "c"), axis=0, tiled=False)

    back, wide = call(
        grad_kernel,
        (
            jax.ShapeDtypeStruct((groups, tiles + 1, toks, LANES), bf16),
            jax.ShapeDtypeStruct((groups * tall, LANES), bf16),
        ),
        whole(4),
        [],
        2 * slots * 2 * LANES * nz * LANES,
        3 << 20,
    )(quad, weight, w_gate[0], w_up[0])
    landed = lax.all_to_all(back, ("y", "xh", "xl", "c"), 0, 0, tiled=True)

    down_grad = call(
        down_kernel,
        jax.ShapeDtypeStruct((LANES, nz * sub), bf16),
        [smem] + whole(ny + 1),
        [rows],
        2 * groups * tall * nz * LANES * LANES,
        4 << 20,
    )(place, *blocks, wide)
    pieces = call(
        functools.partial(sum_kernel, sub),
        jax.ShapeDtypeStruct((nz, OWNERS * toks, LANES), bf16),
        whole(1),
        [pltpu.VMEM((tiles + 1, OWNERS * toks, LANES), f32)],
        groups * toks * nz * LANES,
        1 << 20,
    )(landed.reshape(experts, OWNERS, tiles + 1, toks, LANES))
    final = lax.all_to_all(pieces, "z", 0, 0, tiled=True)
    final = jnp.sum(final.astype(f32), axis=0)
    token_grad = final[:, :sub].reshape(OWNERS, toks, sub).transpose(1, 0, 2).astype(bf16)
    routes = final[:toks, sub:] + final[toks : 2 * toks, sub:]
    route_grad = jnp.sum(jnp.where(onehot, routes[:, None, :], 0.0), axis=2)
    return token_grad, down_grad[None], route_grad


def solution(mesh):
    fine = Mesh(
        mesh.devices.reshape(-1, 2, 2, 2, mesh.devices.shape[1]), ("y", "xh", "xl", "c", "z")
    )
    group = ("y", "xh", "xl", "c")
    return jax.shard_map(
        body,
        mesh=fine,
        in_specs=(
            P(group, None, "z"),
            P(group, None, "z"),
            P(group, None),
            P(group, None),
            P(group, None, "z"),
            P(group, None, "z"),
            P(group, "z", None),
        ),
        out_specs=(P(group, None, "z"), P(group, "z", None), P(group, None)),
        check_vma=False,
    )
```

```python
import functools

import jax
import jax.numpy as jnp
from jax import lax
from jax.experimental import pallas as pl
from jax.experimental.pallas import tpu as pltpu
from jax.sharding import Mesh, PartitionSpec as P

OWNERS = 4
LANES = 128


VMEM_LIMIT = 40 * 1024 * 1024


def hi_lo(v):
    hi = v.astype(jnp.bfloat16).astype(jnp.float32)
    return hi, v - hi


def call(kernel, out_shape, in_specs, scratch, flops, moved):
    return pl.pallas_call(
        kernel,
        out_shape=out_shape,
        in_specs=in_specs,
        out_specs=jax.tree.map(lambda _: pl.BlockSpec(memory_space=pltpu.VMEM), out_shape),
        scratch_shapes=scratch,
        compiler_params=pltpu.CompilerParams(vmem_limit_bytes=VMEM_LIMIT),
        cost_estimate=pl.CostEstimate(flops=flops, bytes_accessed=moved, transcendentals=0),
    )


def whole(count):
    return [pl.BlockSpec(memory_space=pltpu.VMEM)] * count


def upper(shape):
    return lax.broadcasted_iota(jnp.int32, shape, len(shape) - 2) >= 4


def swap(v):
    return pltpu.roll(v, 4, axis=v.ndim - 2)


def first_fours(v):
    pairs = v.reshape(v.shape[0] // 16, 2, 8, v.shape[1])
    even, odd = pairs[:, 0], pairs[:, 1]
    return jnp.where(upper(even.shape), swap(odd), even).reshape(-1, v.shape[1])


def last_fours(v):
    pairs = v.reshape(v.shape[0] // 16, 2, 8, v.shape[1])
    even, odd = pairs[:, 0], pairs[:, 1]
    return jnp.where(upper(even.shape), odd, swap(even)).reshape(-1, v.shape[1])


def block_home(place, index, count):
    offset = jnp.where(place[2] == 0, index, count - index)
    return lax.rem(place[0] + offset, count)


def lay_rows(place, blocks, rows):
    count = len(blocks)
    tiles = rows.shape[1] // LANES
    for index, block in enumerate(blocks):
        per_y = block.shape[0] // tiles
        size = per_y * 8
        base = pl.multiple_of(block_home(place, index, count) * size, size)
        for k in range(tiles):
            tile = block[k * per_y : (k + 1) * per_y].astype(jnp.float32)
            rows[pl.ds(base, size), k * LANES : (k + 1) * LANES] = tile.reshape(
                size, LANES
            ).astype(jnp.bfloat16)


def pack_kernel(sub, got, block):
    f32 = jnp.float32
    per_y, nz, _, _ = got.shape
    size = per_y * 8
    tiles = nz * sub // LANES
    lane = lax.broadcasted_iota(jnp.int32, (size, LANES), 1)
    for k in range(tiles):
        first, skip = divmod(k * LANES, sub)
        tile = got[:, first].astype(f32).reshape(size, LANES)
        if skip:
            tile = pltpu.roll(tile, LANES - skip, axis=1)
        after = got[:, first + 1].astype(f32).reshape(size, LANES)
        after = pltpu.roll(after, sub - skip, axis=1)
        tile = jnp.where(lane < sub - skip, tile, after)
        block[k * per_y : (k + 1) * per_y] = tile.reshape(per_y, 8, LANES).astype(block.dtype)
    width = LANES - sub
    lane = lax.broadcasted_iota(jnp.int32, (8, LANES), 1)
    tags = jnp.zeros((8, LANES), f32)
    for s in range(per_y):
        moved = pltpu.roll(got[s, 0].astype(f32), (width * s - sub) % LANES, axis=1)
        tags = jnp.where((lane >= width * s) & (lane < width * (s + 1)), moved, tags)
    block[tiles * per_y] = tags.astype(block.dtype)


def part_kernel(place, *refs):
    *blocks, gate, up, down_far, part, weight, rows, spread, down, sem = refs
    f32 = jnp.float32
    fetch = pltpu.make_async_copy(down_far, down, sem)
    fetch.start()
    lay_rows(place, blocks, rows)
    mat = rows[...]
    count = len(blocks)
    size = rows.shape[0] // count
    per_y = size // 8
    shape = (per_y, 8, LANES)
    lane = lax.broadcasted_iota(jnp.int32, shape, 2)
    want = place[1] + lax.broadcasted_iota(jnp.int32, shape, 0) * (LANES // per_y)
    for index, block in enumerate(blocks):
        tags = jnp.broadcast_to(block[block.shape[0] - 1].astype(f32)[None], shape)
        tags = jnp.sum(jnp.where(lane == want, tags, 0.0), axis=2, keepdims=True)
        base = pl.multiple_of(block_home(place, index, count) * size, size)
        spread[pl.ds(base, size), :] = jnp.broadcast_to(tags, shape).reshape(size, LANES)
    weight[...] = first_fours(spread[...])
    for index, mats in enumerate((gate, up)):
        out = jnp.dot(mat, mats[...], preferred_element_type=f32)
        part[:, index * LANES : (index + 1) * LANES] = first_fours(out).astype(part.dtype)
    fetch.wait()
    out = lax.dot_general(mat, down[...], (((1,), (1,)), ((), ())), preferred_element_type=f32)
    part[:, 2 * LANES :] = last_fours(out).astype(part.dtype)


def grad_kernel(quad, weight, gate, up, back, wide):
    f32, bf16 = jnp.float32, jnp.bfloat16
    sums = quad[0].astype(f32)
    for index in range(1, OWNERS):
        sums = sums + quad[index].astype(f32)
    gate_pre = sums[:, :LANES]
    up_pre = sums[:, LANES : 2 * LANES]
    hidden_grad = sums[:, 2 * LANES :]
    sig = jax.nn.sigmoid(gate_pre)
    hidden = (gate_pre * sig * up_pre).astype(bf16).astype(f32)
    route = jnp.sum(hidden * hidden_grad, axis=1, keepdims=True)
    scaled = weight[...] * hidden_grad
    gate_grad = (scaled * up_pre * sig * (1.0 + gate_pre * (1.0 - sig))).astype(bf16)
    up_grad = (scaled * gate_pre * sig).astype(bf16)
    route_hi, route_lo = hi_lo(route)
    slots = route.shape[0]
    groups, tiles, toks, _ = back.shape
    lane = lax.broadcasted_iota(jnp.int32, (slots, LANES), 1)
    tags = jnp.where(lane == 0, route_hi, jnp.where(lane == 1, route_lo, 0.0))
    back[:, tiles - 1] = tags.reshape(groups, toks, LANES).astype(bf16)
    across = (((1,), (1,)), ((), ()))
    for k in range(0, tiles - 1, 2):
        cols = slice(k * LANES, (k + 2) * LANES)
        out = lax.dot_general(gate_grad, gate[cols], across, preferred_element_type=f32)
        out = out + lax.dot_general(up_grad, up[cols], across, preferred_element_type=f32)
        for j in range(2):
            tile = out[:, j * LANES : (j + 1) * LANES]
            back[:, k + j] = tile.reshape(groups, toks, LANES).astype(bf16)
    pairs = slots // 8
    weighted = (weight[...] * hidden).reshape(pairs, 8, LANES)
    mask = upper(weighted.shape)
    even = jnp.where(mask, swap(weighted), 0.0)
    odd = jnp.where(mask, weighted, 0.0)
    wide[...] = jnp.stack([even, odd], axis=1).reshape(pairs * 16, LANES).astype(bf16)


def down_kernel(place, *refs):
    *blocks, wide, out, rows = refs
    lay_rows(place, blocks, rows)
    out[...] = lax.dot_general(
        wide[...], rows[...], (((0,), (0,)), ((), ())), preferred_element_type=jnp.float32
    ).astype(out.dtype)


def sum_kernel(sub, landed, pieces, acc):
    f32 = jnp.float32
    experts, owners, tiles, toks, _ = landed.shape
    tags = jnp.zeros((2 * toks, LANES), f32)
    lane = lax.broadcasted_iota(jnp.int32, (toks, LANES), 1)
    tag_hi = jnp.zeros((toks, LANES), f32)
    for e in range(experts):
        pair = landed[e, 0, tiles - 1].astype(f32)
        both = jnp.sum(jnp.where(lane < 2, pair, 0.0), axis=1, keepdims=True)
        tag_hi = jnp.where(lane == sub + e, both, tag_hi)
    tag_hi, tag_lo = hi_lo(tag_hi)
    acc[tiles - 1] = jnp.zeros_like(acc[tiles - 1])
    acc[tiles - 1, :toks] = tag_hi
    acc[tiles - 1, toks : 2 * toks] = tag_lo
    for k in range(tiles - 1):
        for q in range(owners):
            acc[k, q * toks : (q + 1) * toks] = jnp.sum(landed[:, q, k].astype(f32), axis=0)
    tags = acc[tiles - 1]
    lane = lax.broadcasted_iota(jnp.int32, tags.shape, 1)
    for m in range(pieces.shape[0]):
        first, skip = divmod(m * sub, LANES)
        tile = acc[first]
        if skip:
            tile = pltpu.roll(tile, LANES - skip, axis=1)
        if skip + sub > LANES:
            after = pltpu.roll(acc[first + 1], LANES - skip, axis=1)
            tile = jnp.where(lane < LANES - skip, tile, after)
        pieces[m] = jnp.where(lane < sub, tile, tags).astype(pieces.dtype)


def end_kernel(sub, final, ids, token_grad, route_grad, acc):
    f32 = jnp.float32
    toks, owners, _ = token_grad.shape
    acc[...] = jnp.sum(final[...].astype(f32), axis=0)
    for q in range(owners):
        token_grad[:, q, :] = acc[q * toks : (q + 1) * toks, :sub].astype(token_grad.dtype)
    routes = acc[:toks, :] + acc[toks : 2 * toks, :]
    lane = lax.broadcasted_iota(jnp.int32, routes.shape, 1) - sub
    cols = lax.broadcasted_iota(jnp.int32, ids.shape, 1)
    out = jnp.zeros(ids.shape, f32)
    for k in range(ids.shape[1]):
        hit = jnp.sum(jnp.where(lane == ids[:, k : k + 1], routes, 0.0), axis=1, keepdims=True)
        out = jnp.where(cols == k, hit, out)
    route_grad[...] = out


def weight_table(expert_ids, route_weights, experts):
    onehot = expert_ids[:, :, None] == jnp.arange(experts, dtype=jnp.int32)[None, None, :]
    weights = jnp.where(onehot, route_weights.astype(jnp.float32)[:, :, None], 0.0)
    return jnp.sum(weights, axis=1).astype(jnp.bfloat16)


def y_ring(block):
    count = lax.axis_size("y")
    axes = ("y", "c")

    def route(turn):
        hops = []
        for y in range(count):
            for c in range(2):
                step = turn if c == 0 else -turn
                hops.append((2 * y + c, 2 * ((y + step) % count) + c))
        return hops

    blocks = [None] * count
    blocks[0] = block
    fwd = bwd = block
    for step in range(1, count // 2 + 1):
        fwd = lax.ppermute(fwd, axes, route(1))
        blocks[(-step) % count] = fwd
        if step < count // 2:
            bwd = lax.ppermute(bwd, axes, route(-1))
            blocks[step] = bwd
    return blocks


def body(tokens, out_grad, route_weights, expert_ids, w_gate, w_up, w_down):
    f32, bf16 = jnp.float32, jnp.bfloat16
    ny, nxh, nz = lax.axis_size("y"), lax.axis_size("xh"), lax.axis_size("z")
    experts = ny * nxh
    toks, _, sub = tokens.shape
    per_y = nxh * OWNERS
    groups = ny * per_y
    tall = 2 * toks
    my_y = lax.axis_index("y")
    expert = my_y * nxh + lax.axis_index("xh")
    place = jnp.stack([my_y, expert, lax.axis_index("c")]).astype(jnp.int32)

    table = weight_table(expert_ids, route_weights, experts)
    x_rows = jnp.concatenate(
        [tokens.transpose(1, 0, 2), jnp.broadcast_to(table[None], (OWNERS, toks, experts))], axis=2
    )
    g_rows = jnp.pad(out_grad.transpose(1, 0, 2), ((0, 0), (0, 0), (0, LANES - sub)))
    send = jnp.concatenate([x_rows, g_rows], axis=1)
    send = jnp.broadcast_to(send[None, :, None], (nxh, OWNERS, nz, tall, LANES))
    send = send.reshape(nxh * OWNERS * nz, tall, LANES)
    got = lax.all_to_all(send, ("xh", "xl", "c", "z"), 0, 0, tiled=True)
    tiles = nz * sub // LANES
    block = call(
        functools.partial(pack_kernel, sub),
        jax.ShapeDtypeStruct((tiles * per_y + 1, tall, LANES), bf16),
        whole(1),
        [],
        groups * tall * LANES,
        1 << 19,
    )(got.reshape(per_y, nz, tall, LANES))
    blocks = y_ring(block)

    smem = pl.BlockSpec(memory_space=pltpu.SMEM)
    slots = groups * toks
    rows = pltpu.VMEM((groups * tall, nz * sub), bf16)
    part, weight = call(
        part_kernel,
        (
            jax.ShapeDtypeStruct((slots, 3 * LANES), bf16),
            jax.ShapeDtypeStruct((slots, LANES), f32),
        ),
        [smem] + whole(ny + 2) + [pl.BlockSpec(memory_space=pl.ANY)],
        [
            rows,
            pltpu.VMEM((groups * tall, LANES), f32),
            pltpu.VMEM((LANES, nz * sub), bf16),
            pltpu.SemaphoreType.DMA,
        ],
        2 * groups * tall * nz * LANES * 3 * LANES,
        4 << 20,
    )(place, *blocks, w_gate[0], w_up[0], w_down[0])

    quad = lax.all_gather(part, ("xl", "c"), axis=0, tiled=False)

    back, wide = call(
        grad_kernel,
        (
            jax.ShapeDtypeStruct((groups, tiles + 1, toks, LANES), bf16),
            jax.ShapeDtypeStruct((groups * tall, LANES), bf16),
        ),
        whole(4),
        [],
        2 * slots * 2 * LANES * nz * LANES,
        3 << 20,
    )(quad, weight, w_gate[0], w_up[0])
    landed = lax.all_to_all(back, ("y", "xh", "xl", "c"), 0, 0, tiled=True)

    down_grad = call(
        down_kernel,
        jax.ShapeDtypeStruct((LANES, nz * sub), bf16),
        [smem] + whole(ny + 1),
        [rows],
        2 * groups * tall * nz * LANES * LANES,
        4 << 20,
    )(place, *blocks, wide)
    pieces = call(
        functools.partial(sum_kernel, sub),
        jax.ShapeDtypeStruct((nz, OWNERS * toks, LANES), bf16),
        whole(1),
        [pltpu.VMEM((tiles + 1, OWNERS * toks, LANES), f32)],
        groups * toks * nz * LANES,
        1 << 20,
    )(landed.reshape(experts, OWNERS, tiles + 1, toks, LANES))
    final = lax.all_to_all(pieces, "z", 0, 0, tiled=True)
    token_grad, route_grad = call(
        functools.partial(end_kernel, sub),
        (
            jax.ShapeDtypeStruct((toks, OWNERS, sub), bf16),
            jax.ShapeDtypeStruct(expert_ids.shape, f32),
        ),
        whole(2),
        [pltpu.VMEM((OWNERS * toks, LANES), f32)],
        nz * OWNERS * toks * LANES,
        1 << 17,
    )(final, expert_ids)
    return token_grad, down_grad[None], route_grad


def solution(mesh):
    fine = Mesh(
        mesh.devices.reshape(-1, 2, 2, 2, mesh.devices.shape[1]), ("y", "xh", "xl", "c", "z")
    )
    group = ("y", "xh", "xl", "c")
    return jax.shard_map(
        body,
        mesh=fine,
        in_specs=(
            P(group, None, "z"),
            P(group, None, "z"),
            P(group, None),
            P(group, None),
            P(group, None, "z"),
            P(group, None, "z"),
            P(group, "z", None),
        ),
        out_specs=(P(group, None, "z"), P(group, "z", None), P(group, None)),
        check_vma=False,
    )
```

```python
import functools

import jax
import jax.numpy as jnp
from jax import lax
from jax.experimental import pallas as pl
from jax.experimental.pallas import tpu as pltpu
from jax.sharding import Mesh, PartitionSpec as P

OWNERS = 4
LANES = 128


VMEM_LIMIT = 40 * 1024 * 1024


def hi_lo(v):
    hi = v.astype(jnp.bfloat16).astype(jnp.float32)
    return hi, v - hi


def call(kernel, out_shape, in_specs, scratch, flops, moved):
    return pl.pallas_call(
        kernel,
        out_shape=out_shape,
        in_specs=in_specs,
        out_specs=jax.tree.map(lambda _: pl.BlockSpec(memory_space=pltpu.VMEM), out_shape),
        scratch_shapes=scratch,
        compiler_params=pltpu.CompilerParams(vmem_limit_bytes=VMEM_LIMIT),
        cost_estimate=pl.CostEstimate(flops=flops, bytes_accessed=moved, transcendentals=0),
    )


def whole(count):
    return [pl.BlockSpec(memory_space=pltpu.VMEM)] * count


def upper(shape):
    return lax.broadcasted_iota(jnp.int32, shape, len(shape) - 2) >= 4


def swap(v):
    return pltpu.roll(v, 4, axis=v.ndim - 2)


def first_fours(v):
    pairs = v.reshape(v.shape[0] // 16, 2, 8, v.shape[1])
    even, odd = pairs[:, 0], pairs[:, 1]
    return jnp.where(upper(even.shape), swap(odd), even).reshape(-1, v.shape[1])


def last_fours(v):
    pairs = v.reshape(v.shape[0] // 16, 2, 8, v.shape[1])
    even, odd = pairs[:, 0], pairs[:, 1]
    return jnp.where(upper(even.shape), odd, swap(even)).reshape(-1, v.shape[1])


def block_offsets(count):
    offsets = [0, 1]
    for step in range(1, count // 2):
        if step % 2:
            offsets += [-step, -step - 1]
        else:
            offsets += [step, step + 1]
    return offsets


def block_home(place, index, count):
    offset = block_offsets(count)[index]
    return lax.rem(place[0] + place[2] * offset + count, count)


def split_blocks(refs):
    blocks = list(refs[:2])
    for ref in refs[2:]:
        blocks += [ref.at[0], ref.at[1]]
    return blocks


def lay_rows(place, blocks, rows):
    count = len(blocks)
    tiles = rows.shape[1] // LANES
    for index, block in enumerate(blocks):
        per_y = block.shape[0] // tiles
        size = per_y * 8
        base = pl.multiple_of(block_home(place, index, count) * size, size)
        for k in range(tiles):
            tile = block[k * per_y : (k + 1) * per_y].astype(jnp.float32)
            rows[pl.ds(base, size), k * LANES : (k + 1) * LANES] = tile.reshape(
                size, LANES
            ).astype(jnp.bfloat16)


def pack_kernel(sub, got, block):
    f32 = jnp.float32
    per_y, nz, _, _ = got.shape
    size = per_y * 8
    tiles = nz * sub // LANES
    lane = lax.broadcasted_iota(jnp.int32, (size, LANES), 1)
    for k in range(tiles):
        first, skip = divmod(k * LANES, sub)
        tile = got[:, first].astype(f32).reshape(size, LANES)
        if skip:
            tile = pltpu.roll(tile, LANES - skip, axis=1)
        after = got[:, first + 1].astype(f32).reshape(size, LANES)
        after = pltpu.roll(after, sub - skip, axis=1)
        tile = jnp.where(lane < sub - skip, tile, after)
        block[k * per_y : (k + 1) * per_y] = tile.reshape(per_y, 8, LANES).astype(block.dtype)
    width = LANES - sub
    lane = lax.broadcasted_iota(jnp.int32, (8, LANES), 1)
    tags = jnp.zeros((8, LANES), f32)
    for s in range(per_y):
        moved = pltpu.roll(got[s, 0].astype(f32), (width * s - sub) % LANES, axis=1)
        tags = jnp.where((lane >= width * s) & (lane < width * (s + 1)), moved, tags)
    block[tiles * per_y] = tags.astype(block.dtype)


def part_kernel(place, *refs):
    *blocks, gate, up, down, part, weight, rows, spread = refs
    blocks = split_blocks(blocks)
    f32 = jnp.float32
    lay_rows(place, blocks, rows)
    mat = rows[...]
    count = len(blocks)
    size = rows.shape[0] // count
    per_y = size // 8
    shape = (per_y, 8, LANES)
    lane = lax.broadcasted_iota(jnp.int32, shape, 2)
    want = place[1] + lax.broadcasted_iota(jnp.int32, shape, 0) * (LANES // per_y)
    for index, block in enumerate(blocks):
        tags = jnp.broadcast_to(block[block.shape[0] - 1].astype(f32)[None], shape)
        tags = jnp.sum(jnp.where(lane == want, tags, 0.0), axis=2, keepdims=True)
        base = pl.multiple_of(block_home(place, index, count) * size, size)
        spread[pl.ds(base, size), :] = jnp.broadcast_to(tags, shape).reshape(size, LANES)
    weight[...] = first_fours(spread[...])
    for index, mats in enumerate((gate, up)):
        out = jnp.dot(mat, mats[...], preferred_element_type=f32)
        part[:, index * LANES : (index + 1) * LANES] = first_fours(out).astype(part.dtype)
    out = lax.dot_general(mat, down[...], (((1,), (1,)), ((), ())), preferred_element_type=f32)
    part[:, 2 * LANES :] = last_fours(out).astype(part.dtype)


def grad_kernel(quad, weight, gate, up, back, wide):
    f32, bf16 = jnp.float32, jnp.bfloat16
    sums = quad[0].astype(f32)
    for index in range(1, OWNERS):
        sums = sums + quad[index].astype(f32)
    gate_pre = sums[:, :LANES]
    up_pre = sums[:, LANES : 2 * LANES]
    hidden_grad = sums[:, 2 * LANES :]
    sig = jax.nn.sigmoid(gate_pre)
    hidden = (gate_pre * sig * up_pre).astype(bf16).astype(f32)
    route = jnp.sum(hidden * hidden_grad, axis=1, keepdims=True)
    scaled = weight[...] * hidden_grad
    gate_grad = (scaled * up_pre * sig * (1.0 + gate_pre * (1.0 - sig))).astype(bf16)
    up_grad = (scaled * gate_pre * sig).astype(bf16)
    route_hi, route_lo = hi_lo(route)
    slots = route.shape[0]
    groups, tiles, toks, _ = back.shape
    lane = lax.broadcasted_iota(jnp.int32, (slots, LANES), 1)
    tags = jnp.where(lane == 0, route_hi, jnp.where(lane == 1, route_lo, 0.0))
    back[:, tiles - 1] = tags.reshape(groups, toks, LANES).astype(bf16)
    across = (((1,), (1,)), ((), ()))
    for k in range(0, tiles - 1, 2):
        cols = slice(k * LANES, (k + 2) * LANES)
        out = lax.dot_general(gate_grad, gate[cols], across, preferred_element_type=f32)
        out = out + lax.dot_general(up_grad, up[cols], across, preferred_element_type=f32)
        for j in range(2):
            tile = out[:, j * LANES : (j + 1) * LANES]
            back[:, k + j] = tile.reshape(groups, toks, LANES).astype(bf16)
    pairs = slots // 8
    weighted = (weight[...] * hidden).reshape(pairs, 8, LANES)
    mask = upper(weighted.shape)
    even = jnp.where(mask, swap(weighted), 0.0)
    odd = jnp.where(mask, weighted, 0.0)
    wide[...] = jnp.stack([even, odd], axis=1).reshape(pairs * 16, LANES).astype(bf16)


def down_kernel(place, *refs):
    *blocks, wide, out, rows = refs
    blocks = split_blocks(blocks)
    lay_rows(place, blocks, rows)
    out[...] = lax.dot_general(
        wide[...], rows[...], (((0,), (0,)), ((), ())), preferred_element_type=jnp.float32
    ).astype(out.dtype)


def sum_kernel(sub, landed, pieces, acc):
    f32 = jnp.float32
    experts, owners, tiles, toks, _ = landed.shape
    tags = jnp.zeros((2 * toks, LANES), f32)
    lane = lax.broadcasted_iota(jnp.int32, (toks, LANES), 1)
    tag_hi = jnp.zeros((toks, LANES), f32)
    for e in range(experts):
        pair = landed[e, 0, tiles - 1].astype(f32)
        both = jnp.sum(jnp.where(lane < 2, pair, 0.0), axis=1, keepdims=True)
        tag_hi = jnp.where(lane == sub + e, both, tag_hi)
    tag_hi, tag_lo = hi_lo(tag_hi)
    acc[tiles - 1] = jnp.zeros_like(acc[tiles - 1])
    acc[tiles - 1, :toks] = tag_hi
    acc[tiles - 1, toks : 2 * toks] = tag_lo
    for k in range(tiles - 1):
        for q in range(owners):
            acc[k, q * toks : (q + 1) * toks] = jnp.sum(landed[:, q, k].astype(f32), axis=0)
    tags = acc[tiles - 1]
    lane = lax.broadcasted_iota(jnp.int32, tags.shape, 1)
    for m in range(pieces.shape[0]):
        first, skip = divmod(m * sub, LANES)
        tile = acc[first]
        if skip:
            tile = pltpu.roll(tile, LANES - skip, axis=1)
        if skip + sub > LANES:
            after = pltpu.roll(acc[first + 1], LANES - skip, axis=1)
            tile = jnp.where(lane < LANES - skip, tile, after)
        pieces[m] = jnp.where(lane < sub, tile, tags).astype(pieces.dtype)


def end_kernel(sub, final, ids, token_grad, route_grad, acc):
    f32 = jnp.float32
    toks, owners, _ = token_grad.shape
    acc[...] = jnp.sum(final[...].astype(f32), axis=0)
    for q in range(owners):
        token_grad[:, q, :] = acc[q * toks : (q + 1) * toks, :sub].astype(token_grad.dtype)
    routes = acc[:toks, :] + acc[toks : 2 * toks, :]
    lane = lax.broadcasted_iota(jnp.int32, routes.shape, 1) - sub
    cols = lax.broadcasted_iota(jnp.int32, ids.shape, 1)
    out = jnp.zeros(ids.shape, f32)
    for k in range(ids.shape[1]):
        hit = jnp.sum(jnp.where(lane == ids[:, k : k + 1], routes, 0.0), axis=1, keepdims=True)
        out = jnp.where(cols == k, hit, out)
    route_grad[...] = out


def weight_table(expert_ids, route_weights, experts):
    onehot = expert_ids[:, :, None] == jnp.arange(experts, dtype=jnp.int32)[None, None, :]
    weights = jnp.where(onehot, route_weights.astype(jnp.float32)[:, :, None], 0.0)
    return jnp.sum(weights, axis=1).astype(jnp.bfloat16)


def swap_with(block, toward):
    count = lax.axis_size("y")
    hops = []
    for y in range(count):
        for c in range(2):
            step = 1 if (y + c) % 2 == 0 else -1
            step = step if toward else -step
            hops.append((2 * y + c, 2 * ((y + step) % count) + c))
    return lax.ppermute(block, ("y", "c"), hops)


def y_gather(block):
    first = swap_with(block, True)
    pair = swap_with(jnp.stack([block, first]), False)
    found = [block, first, pair]
    for step in range(2, lax.axis_size("y") // 2):
        pair = swap_with(pair, step % 2 == 0)
        found.append(pair)
    return found


def body(tokens, out_grad, route_weights, expert_ids, w_gate, w_up, w_down):
    f32, bf16 = jnp.float32, jnp.bfloat16
    ny, nxh, nz = lax.axis_size("y"), lax.axis_size("xh"), lax.axis_size("z")
    experts = ny * nxh
    toks, _, sub = tokens.shape
    per_y = nxh * OWNERS
    groups = ny * per_y
    tall = 2 * toks
    my_y = lax.axis_index("y")
    expert = my_y * nxh + lax.axis_index("xh")
    turn = 1 - 2 * lax.rem(my_y + lax.axis_index("c"), 2)
    place = jnp.stack([my_y, expert, turn]).astype(jnp.int32)

    table = weight_table(expert_ids, route_weights, experts)
    x_rows = jnp.concatenate(
        [tokens.transpose(1, 0, 2), jnp.broadcast_to(table[None], (OWNERS, toks, experts))], axis=2
    )
    g_rows = jnp.pad(out_grad.transpose(1, 0, 2), ((0, 0), (0, 0), (0, LANES - sub)))
    send = jnp.concatenate([x_rows, g_rows], axis=1)
    send = jnp.broadcast_to(send[None, :, None], (nxh, OWNERS, nz, tall, LANES))
    send = send.reshape(nxh * OWNERS * nz, tall, LANES)
    got = lax.all_to_all(send, ("xh", "xl", "c", "z"), 0, 0, tiled=True)
    tiles = nz * sub // LANES
    block = call(
        functools.partial(pack_kernel, sub),
        jax.ShapeDtypeStruct((tiles * per_y + 1, tall, LANES), bf16),
        whole(1),
        [],
        groups * tall * LANES,
        1 << 19,
    )(got.reshape(per_y, nz, tall, LANES))
    blocks = y_gather(block)

    smem = pl.BlockSpec(memory_space=pltpu.SMEM)
    slots = groups * toks
    rows = pltpu.VMEM((groups * tall, nz * sub), bf16)
    part, weight = call(
        part_kernel,
        (
            jax.ShapeDtypeStruct((slots, 3 * LANES), bf16),
            jax.ShapeDtypeStruct((slots, LANES), f32),
        ),
        [smem] + whole(len(blocks) + 3),
        [rows, pltpu.VMEM((groups * tall, LANES), f32)],
        2 * groups * tall * nz * LANES * 3 * LANES,
        4 << 20,
    )(place, *blocks, w_gate[0], w_up[0], w_down[0])

    quad = lax.all_gather(part, ("xl", "c"), axis=0, tiled=False)

    back, wide = call(
        grad_kernel,
        (
            jax.ShapeDtypeStruct((groups, tiles + 1, toks, LANES), bf16),
            jax.ShapeDtypeStruct((groups * tall, LANES), bf16),
        ),
        whole(4),
        [],
        2 * slots * 2 * LANES * nz * LANES,
        3 << 20,
    )(quad, weight, w_gate[0], w_up[0])
    landed = lax.all_to_all(back, ("y", "xh", "xl", "c"), 0, 0, tiled=True)

    down_grad = call(
        down_kernel,
        jax.ShapeDtypeStruct((LANES, nz * sub), bf16),
        [smem] + whole(len(blocks) + 1),
        [rows],
        2 * groups * tall * nz * LANES * LANES,
        4 << 20,
    )(place, *blocks, wide)
    pieces = call(
        functools.partial(sum_kernel, sub),
        jax.ShapeDtypeStruct((nz, OWNERS * toks, LANES), bf16),
        whole(1),
        [pltpu.VMEM((tiles + 1, OWNERS * toks, LANES), f32)],
        groups * toks * nz * LANES,
        1 << 20,
    )(landed.reshape(experts, OWNERS, tiles + 1, toks, LANES))
    final = lax.all_to_all(pieces, "z", 0, 0, tiled=True)
    token_grad, route_grad = call(
        functools.partial(end_kernel, sub),
        (
            jax.ShapeDtypeStruct((toks, OWNERS, sub), bf16),
            jax.ShapeDtypeStruct(expert_ids.shape, f32),
        ),
        whole(2),
        [pltpu.VMEM((OWNERS * toks, LANES), f32)],
        nz * OWNERS * toks * LANES,
        1 << 17,
    )(final, expert_ids)
    return token_grad, down_grad[None], route_grad


def solution(mesh):
    fine = Mesh(
        mesh.devices.reshape(-1, 2, 2, 2, mesh.devices.shape[1]), ("y", "xh", "xl", "c", "z")
    )
    group = ("y", "xh", "xl", "c")
    return jax.shard_map(
        body,
        mesh=fine,
        in_specs=(
            P(group, None, "z"),
            P(group, None, "z"),
            P(group, None),
            P(group, None),
            P(group, None, "z"),
            P(group, None, "z"),
            P(group, "z", None),
        ),
        out_specs=(P(group, None, "z"), P(group, "z", None), P(group, None)),
        check_vma=False,
    )
```

```python
import functools

import jax
import jax.numpy as jnp
from jax import lax
from jax.experimental import pallas as pl
from jax.experimental.pallas import tpu as pltpu
from jax.sharding import Mesh, PartitionSpec as P

OWNERS = 4
LANES = 128


VMEM_LIMIT = 40 * 1024 * 1024
BLOCK_PICKS = ((0, None), (1, None), (2, 0), (2, 1), (3, 0), (3, 1), (4, 0), (4, 1))
BLOCK_OFFSETS = (0, 1, -1, -2, 2, 3, -3, -4)
BLOCK_ORDER = (0, 1, -1, 2, -2, 3, -3, 4)
PART_FLOPS = 4 * 10**9


def hi_lo(v):
    hi = v.astype(jnp.bfloat16).astype(jnp.float32)
    return hi, v - hi


def call(kernel, out_shape, in_specs, scratch, flops, moved):
    return pl.pallas_call(
        kernel,
        out_shape=out_shape,
        in_specs=in_specs,
        out_specs=jax.tree.map(lambda _: pl.BlockSpec(memory_space=pltpu.VMEM), out_shape),
        scratch_shapes=scratch,
        compiler_params=pltpu.CompilerParams(vmem_limit_bytes=VMEM_LIMIT),
        cost_estimate=pl.CostEstimate(flops=flops, bytes_accessed=moved, transcendentals=0),
    )


def whole(count):
    return [pl.BlockSpec(memory_space=pltpu.VMEM)] * count


def upper(shape):
    return lax.broadcasted_iota(jnp.int32, shape, len(shape) - 2) >= 4


def swap(v):
    return pltpu.roll(v, 4, axis=v.ndim - 2)


def first_fours(v):
    pairs = v.reshape(v.shape[0] // 16, 2, 8, v.shape[1])
    even, odd = pairs[:, 0], pairs[:, 1]
    return jnp.where(upper(even.shape), swap(odd), even).reshape(-1, v.shape[1])


def last_fours(v):
    pairs = v.reshape(v.shape[0] // 16, 2, 8, v.shape[1])
    even, odd = pairs[:, 0], pairs[:, 1]
    return jnp.where(upper(even.shape), odd, swap(even)).reshape(-1, v.shape[1])


def block_offsets(count):
    offsets = [0, 1]
    for step in range(1, count // 2):
        if step % 2:
            offsets += [-step, -step - 1]
        else:
            offsets += [step, step + 1]
    return offsets


def lay_rows(turn, blocks, offsets, first, rows):
    tiles = rows.shape[1] // LANES
    for block, offset in zip(blocks, offsets):
        per_y = block.shape[0] // tiles
        size = per_y * 8
        base = pl.multiple_of(row_place(turn, offset, first) * size, size)
        for k in range(tiles):
            tile = block[k * per_y : (k + 1) * per_y].astype(jnp.float32)
            rows[pl.ds(base, size), k * LANES : (k + 1) * LANES] = tile.reshape(
                size, LANES
            ).astype(jnp.bfloat16)


def row_place(turn, offset, first):
    if offset == 0:
        return 0
    if offset == -4:
        return 7 - first
    ahead = turn if offset > 0 else -turn
    return 2 * abs(offset) - 1 - first + jnp.where(ahead > 0, 0, 1)


def pack_kernel(sub, got, block):
    f32 = jnp.float32
    per_y, nz, _, _ = got.shape
    size = per_y * 8
    tiles = nz * sub // LANES
    lane = lax.broadcasted_iota(jnp.int32, (size, LANES), 1)
    for k in range(tiles):
        first, skip = divmod(k * LANES, sub)
        tile = got[:, first].astype(f32).reshape(size, LANES)
        if skip:
            tile = pltpu.roll(tile, LANES - skip, axis=1)
        after = got[:, first + 1].astype(f32).reshape(size, LANES)
        after = pltpu.roll(after, sub - skip, axis=1)
        tile = jnp.where(lane < sub - skip, tile, after)
        block[k * per_y : (k + 1) * per_y] = tile.reshape(per_y, 8, LANES).astype(block.dtype)
    width = LANES - sub
    lane = lax.broadcasted_iota(jnp.int32, (8, LANES), 1)
    tags = jnp.zeros((8, LANES), f32)
    for s in range(per_y):
        moved = pltpu.roll(got[s, 0].astype(f32), (width * s - sub) % LANES, axis=1)
        tags = jnp.where((lane >= width * s) & (lane < width * (s + 1)), moved, tags)
    block[tiles * per_y] = tags.astype(block.dtype)


def part_kernel(picks, offsets, first, place, *refs):
    *found, gate, up, down, part, weight, rows, spread = refs
    blocks = [found[i] if j is None else found[i].at[j] for i, j in picks]
    f32 = jnp.float32
    lay_rows(place[2], blocks, offsets, first, rows)
    mat = rows[...]
    size = rows.shape[0] // len(blocks)
    per_y = size // 8
    shape = (per_y, 8, LANES)
    lane = lax.broadcasted_iota(jnp.int32, shape, 2)
    want = place[1] + lax.broadcasted_iota(jnp.int32, shape, 0) * (LANES // per_y)
    for block, offset in zip(blocks, offsets):
        tags = jnp.broadcast_to(block[block.shape[0] - 1].astype(f32)[None], shape)
        tags = jnp.sum(jnp.where(lane == want, tags, 0.0), axis=2, keepdims=True)
        base = pl.multiple_of(row_place(place[2], offset, first) * size, size)
        spread[pl.ds(base, size), :] = jnp.broadcast_to(tags, shape).reshape(size, LANES)
    weight[...] = first_fours(spread[...])
    for index, mats in enumerate((gate, up)):
        out = jnp.dot(mat, mats[...], preferred_element_type=f32)
        part[:, index * LANES : (index + 1) * LANES] = first_fours(out).astype(part.dtype)
    out = lax.dot_general(mat, down[...], (((1,), (1,)), ((), ())), preferred_element_type=f32)
    part[:, 2 * LANES :] = last_fours(out).astype(part.dtype)


def grad_kernel(place, *refs):
    *pieces, gate, up, back, wide = refs
    f32, bf16 = jnp.float32, jnp.bfloat16
    quads, weights = pieces[: len(pieces) // 2], pieces[len(pieces) // 2 :]
    sums = []
    for quad in quads:
        total = quad[0].astype(f32)
        for index in range(1, OWNERS):
            total = total + quad[index].astype(f32)
        sums.append(total)
    sums = jnp.concatenate(sums, axis=0)
    weight = jnp.concatenate([w[...] for w in weights], axis=0)
    gate_pre = sums[:, :LANES]
    up_pre = sums[:, LANES : 2 * LANES]
    hidden_grad = sums[:, 2 * LANES :]
    sig = jax.nn.sigmoid(gate_pre)
    hidden = (gate_pre * sig * up_pre).astype(bf16).astype(f32)
    route = jnp.sum(hidden * hidden_grad, axis=1, keepdims=True)
    scaled = weight * hidden_grad
    gate_grad = (scaled * up_pre * sig * (1.0 + gate_pre * (1.0 - sig))).astype(bf16)
    up_grad = (scaled * gate_pre * sig).astype(bf16)
    route_hi, route_lo = hi_lo(route)
    slots = route.shape[0]
    groups, tiles, toks, _ = back.shape
    lane = lax.broadcasted_iota(jnp.int32, (slots, LANES), 1)
    tags = jnp.where(lane == 0, route_hi, jnp.where(lane == 1, route_lo, 0.0))
    count = len(BLOCK_ORDER)
    per_y = groups // count
    homes = [
        pl.multiple_of(lax.rem(place[0] + slot + count, count) * per_y, per_y)
        for slot in BLOCK_ORDER
    ]

    def put(k, tile):
        tile = tile.reshape(groups, toks, LANES).astype(bf16)
        for index, home in enumerate(homes):
            back[pl.ds(home, per_y), k] = tile[index * per_y : (index + 1) * per_y]

    put(tiles - 1, tags)
    across = (((1,), (1,)), ((), ()))
    for k in range(0, tiles - 1, 2):
        cols = slice(k * LANES, (k + 2) * LANES)
        out = lax.dot_general(gate_grad, gate[cols], across, preferred_element_type=f32)
        out = out + lax.dot_general(up_grad, up[cols], across, preferred_element_type=f32)
        for j in range(2):
            put(k + j, out[:, j * LANES : (j + 1) * LANES])
    pairs = slots // 8
    weighted = (weight * hidden).reshape(pairs, 8, LANES)
    mask = upper(weighted.shape)
    even = jnp.where(mask, swap(weighted), 0.0)
    odd = jnp.where(mask, weighted, 0.0)
    wide[...] = jnp.stack([even, odd], axis=1).reshape(pairs * 16, LANES).astype(bf16)


def down_kernel(place, *refs):
    *found, wide, out, rows = refs
    blocks = [found[i] if j is None else found[i].at[j] for i, j in BLOCK_PICKS]
    lay_rows(place[2], blocks, BLOCK_OFFSETS, 0, rows)
    out[...] = lax.dot_general(
        wide[...], rows[...], (((0,), (0,)), ((), ())), preferred_element_type=jnp.float32
    ).astype(out.dtype)


def sum_kernel(sub, landed, pieces, acc):
    f32 = jnp.float32
    experts, owners, tiles, toks, _ = landed.shape
    tags = jnp.zeros((2 * toks, LANES), f32)
    lane = lax.broadcasted_iota(jnp.int32, (toks, LANES), 1)
    tag_hi = jnp.zeros((toks, LANES), f32)
    for e in range(experts):
        pair = landed[e, 0, tiles - 1].astype(f32)
        both = jnp.sum(jnp.where(lane < 2, pair, 0.0), axis=1, keepdims=True)
        tag_hi = jnp.where(lane == sub + e, both, tag_hi)
    tag_hi, tag_lo = hi_lo(tag_hi)
    acc[tiles - 1] = jnp.zeros_like(acc[tiles - 1])
    acc[tiles - 1, :toks] = tag_hi
    acc[tiles - 1, toks : 2 * toks] = tag_lo
    for k in range(tiles - 1):
        for q in range(owners):
            acc[k, q * toks : (q + 1) * toks] = jnp.sum(landed[:, q, k].astype(f32), axis=0)
    tags = acc[tiles - 1]
    lane = lax.broadcasted_iota(jnp.int32, tags.shape, 1)
    for m in range(pieces.shape[0]):
        first, skip = divmod(m * sub, LANES)
        tile = acc[first]
        if skip:
            tile = pltpu.roll(tile, LANES - skip, axis=1)
        if skip + sub > LANES:
            after = pltpu.roll(acc[first + 1], LANES - skip, axis=1)
            tile = jnp.where(lane < LANES - skip, tile, after)
        pieces[m] = jnp.where(lane < sub, tile, tags).astype(pieces.dtype)


def end_kernel(sub, final, ids, token_grad, route_grad, acc):
    f32 = jnp.float32
    toks, owners, _ = token_grad.shape
    acc[...] = jnp.sum(final[...].astype(f32), axis=0)
    for q in range(owners):
        token_grad[:, q, :] = acc[q * toks : (q + 1) * toks, :sub].astype(token_grad.dtype)
    routes = acc[:toks, :] + acc[toks : 2 * toks, :]
    lane = lax.broadcasted_iota(jnp.int32, routes.shape, 1) - sub
    cols = lax.broadcasted_iota(jnp.int32, ids.shape, 1)
    out = jnp.zeros(ids.shape, f32)
    for k in range(ids.shape[1]):
        hit = jnp.sum(jnp.where(lane == ids[:, k : k + 1], routes, 0.0), axis=1, keepdims=True)
        out = jnp.where(cols == k, hit, out)
    route_grad[...] = out


def weight_table(expert_ids, route_weights, experts):
    onehot = expert_ids[:, :, None] == jnp.arange(experts, dtype=jnp.int32)[None, None, :]
    weights = jnp.where(onehot, route_weights.astype(jnp.float32)[:, :, None], 0.0)
    return jnp.sum(weights, axis=1).astype(jnp.bfloat16)


def swap_with(block, toward):
    count = lax.axis_size("y")
    hops = []
    for y in range(count):
        for c in range(2):
            step = 1 if (y + c) % 2 == 0 else -1
            step = step if toward else -step
            hops.append((2 * y + c, 2 * ((y + step) % count) + c))
    return lax.ppermute(block, ("y", "c"), hops)


def body(tokens, out_grad, route_weights, expert_ids, w_gate, w_up, w_down):
    f32, bf16 = jnp.float32, jnp.bfloat16
    ny, nxh, nz = lax.axis_size("y"), lax.axis_size("xh"), lax.axis_size("z")
    experts = ny * nxh
    toks, _, sub = tokens.shape
    per_y = nxh * OWNERS
    groups = ny * per_y
    tall = 2 * toks
    my_y = lax.axis_index("y")
    expert = my_y * nxh + lax.axis_index("xh")
    turn = 1 - 2 * lax.rem(my_y + lax.axis_index("c"), 2)
    place = jnp.stack([my_y, expert, turn]).astype(jnp.int32)

    table = weight_table(expert_ids, route_weights, experts)
    x_rows = jnp.concatenate(
        [tokens.transpose(1, 0, 2), jnp.broadcast_to(table[None], (OWNERS, toks, experts))], axis=2
    )
    g_rows = jnp.pad(out_grad.transpose(1, 0, 2), ((0, 0), (0, 0), (0, LANES - sub)))
    send = jnp.concatenate([x_rows, g_rows], axis=1)
    send = jnp.broadcast_to(send[None, :, None], (nxh, OWNERS, nz, tall, LANES))
    send = send.reshape(nxh * OWNERS * nz, tall, LANES)
    got = lax.all_to_all(send, ("xh", "xl", "c", "z"), 0, 0, tiled=True)
    tiles = nz * sub // LANES
    block = call(
        functools.partial(pack_kernel, sub),
        jax.ShapeDtypeStruct((tiles * per_y + 1, tall, LANES), bf16),
        whole(1),
        [],
        groups * tall * LANES,
        1 << 19,
    )(got.reshape(per_y, nz, tall, LANES))
    smem = pl.BlockSpec(memory_space=pltpu.SMEM)
    slots = groups * toks
    size = per_y * tall
    width = nz * sub

    def partial_sums(found, low, high, first):
        picks = BLOCK_PICKS[low:high] if first != 3 else (BLOCK_PICKS[3], BLOCK_PICKS[4])
        used = sorted({i for i, _ in picks})
        local = tuple((used.index(i), j) for i, j in picks)
        n = len(picks)
        part, weight = call(
            functools.partial(part_kernel, local, BLOCK_OFFSETS[low:high], first),
            (
                jax.ShapeDtypeStruct((n * per_y * toks, 3 * LANES), bf16),
                jax.ShapeDtypeStruct((n * per_y * toks, LANES), f32),
            ),
            [smem] + whole(len(used) + 3),
            [pltpu.VMEM((n * size, width), bf16), pltpu.VMEM((n * size, LANES), f32)],
            PART_FLOPS,
            4 << 20,
        )(place, *[found[i] for i in used], w_gate[0], w_up[0], w_down[0])
        return lax.all_gather(part, ("xl", "c"), axis=0, tiled=False), weight

    first = swap_with(block, True)
    second = swap_with(jnp.stack([block, first]), False)
    third = swap_with(second, True)
    quad_a, weight_a = partial_sums([block, first, second], 0, 3, 0)
    third, quad_a = lax.optimization_barrier((third, quad_a))
    fourth = swap_with(third, False)
    found = [block, first, second, third, fourth]
    quad_b, weight_b = partial_sums(found, 3, 5, 3)
    fourth, quad_b = lax.optimization_barrier((fourth, quad_b))
    found[4] = fourth
    quad_c, weight_c = partial_sums(found, 5, 8, 5)

    back, wide = call(
        grad_kernel,
        (
            jax.ShapeDtypeStruct((groups, tiles + 1, toks, LANES), bf16),
            jax.ShapeDtypeStruct((groups * tall, LANES), bf16),
        ),
        [smem] + whole(8),
        [],
        2 * slots * 2 * LANES * nz * LANES,
        3 << 20,
    )(place, quad_a, quad_b, quad_c, weight_a, weight_b, weight_c, w_gate[0], w_up[0])
    landed = lax.all_to_all(back, ("y", "xh", "xl", "c"), 0, 0, tiled=True)

    down_grad = call(
        down_kernel,
        jax.ShapeDtypeStruct((LANES, nz * sub), bf16),
        [smem] + whole(len(found) + 1),
        [pltpu.VMEM((groups * tall, width), bf16)],
        2 * groups * tall * nz * LANES * LANES,
        4 << 20,
    )(place, *found, wide)
    pieces = call(
        functools.partial(sum_kernel, sub),
        jax.ShapeDtypeStruct((nz, OWNERS * toks, LANES), bf16),
        whole(1),
        [pltpu.VMEM((tiles + 1, OWNERS * toks, LANES), f32)],
        groups * toks * nz * LANES,
        1 << 20,
    )(landed.reshape(experts, OWNERS, tiles + 1, toks, LANES))
    final = lax.all_to_all(pieces, "z", 0, 0, tiled=True)
    token_grad, route_grad = call(
        functools.partial(end_kernel, sub),
        (
            jax.ShapeDtypeStruct((toks, OWNERS, sub), bf16),
            jax.ShapeDtypeStruct(expert_ids.shape, f32),
        ),
        whole(2),
        [pltpu.VMEM((OWNERS * toks, LANES), f32)],
        nz * OWNERS * toks * LANES,
        1 << 17,
    )(final, expert_ids)
    return token_grad, down_grad[None], route_grad


def solution(mesh):
    fine = Mesh(
        mesh.devices.reshape(-1, 2, 2, 2, mesh.devices.shape[1]), ("y", "xh", "xl", "c", "z")
    )
    group = ("y", "xh", "xl", "c")
    return jax.shard_map(
        body,
        mesh=fine,
        in_specs=(
            P(group, None, "z"),
            P(group, None, "z"),
            P(group, None),
            P(group, None),
            P(group, None, "z"),
            P(group, None, "z"),
            P(group, "z", None),
        ),
        out_specs=(P(group, None, "z"), P(group, "z", None), P(group, None)),
        check_vma=False,
    )
```

```python
import functools

import jax
import jax.numpy as jnp
from jax import lax
from jax.experimental import pallas as pl
from jax.experimental.pallas import tpu as pltpu
from jax.sharding import Mesh, PartitionSpec as P

OWNERS = 4
LANES = 128


VMEM_LIMIT = 40 * 1024 * 1024
BLOCK_PICKS = ((0, None), (1, None), (2, None), (3, None), (4, 0), (4, 1), (5, 0), (5, 1))
BLOCK_OFFSETS = (0, 1, -1, -2, 2, 3, -3, -4)
BLOCK_ORDER = (0, 1, -1, 2, -2, 3, -3, 4)
PART_FLOPS = 4 * 10**9


def hi_lo(v):
    hi = v.astype(jnp.bfloat16).astype(jnp.float32)
    return hi, v - hi


def call(kernel, out_shape, in_specs, scratch, flops, moved):
    return pl.pallas_call(
        kernel,
        out_shape=out_shape,
        in_specs=in_specs,
        out_specs=jax.tree.map(lambda _: pl.BlockSpec(memory_space=pltpu.VMEM), out_shape),
        scratch_shapes=scratch,
        compiler_params=pltpu.CompilerParams(vmem_limit_bytes=VMEM_LIMIT),
        cost_estimate=pl.CostEstimate(flops=flops, bytes_accessed=moved, transcendentals=0),
    )


def whole(count):
    return [pl.BlockSpec(memory_space=pltpu.VMEM)] * count


def upper(shape):
    return lax.broadcasted_iota(jnp.int32, shape, len(shape) - 2) >= 4


def swap(v):
    return pltpu.roll(v, 4, axis=v.ndim - 2)


def first_fours(v):
    pairs = v.reshape(v.shape[0] // 16, 2, 8, v.shape[1])
    even, odd = pairs[:, 0], pairs[:, 1]
    return jnp.where(upper(even.shape), swap(odd), even).reshape(-1, v.shape[1])


def last_fours(v):
    pairs = v.reshape(v.shape[0] // 16, 2, 8, v.shape[1])
    even, odd = pairs[:, 0], pairs[:, 1]
    return jnp.where(upper(even.shape), odd, swap(even)).reshape(-1, v.shape[1])


def block_offsets(count):
    offsets = [0, 1]
    for step in range(1, count // 2):
        if step % 2:
            offsets += [-step, -step - 1]
        else:
            offsets += [step, step + 1]
    return offsets


def lay_rows(turn, blocks, offsets, first, rows):
    tiles = rows.shape[1] // LANES
    for block, offset in zip(blocks, offsets):
        per_y = block.shape[0] // tiles
        size = per_y * 8
        base = pl.multiple_of(row_place(turn, offset, first) * size, size)
        for k in range(tiles):
            tile = block[k * per_y : (k + 1) * per_y].astype(jnp.float32)
            rows[pl.ds(base, size), k * LANES : (k + 1) * LANES] = tile.reshape(
                size, LANES
            ).astype(jnp.bfloat16)


def row_place(turn, offset, first):
    if offset == 0:
        return 0
    if offset == -4:
        return 7 - first
    ahead = turn if offset > 0 else -turn
    return 2 * abs(offset) - 1 - first + jnp.where(ahead > 0, 0, 1)


def pack_kernel(sub, got, block):
    f32 = jnp.float32
    per_y, nz, _, _ = got.shape
    size = per_y * 8
    tiles = nz * sub // LANES
    lane = lax.broadcasted_iota(jnp.int32, (size, LANES), 1)
    for k in range(tiles):
        first, skip = divmod(k * LANES, sub)
        tile = got[:, first].astype(f32).reshape(size, LANES)
        if skip:
            tile = pltpu.roll(tile, LANES - skip, axis=1)
        after = got[:, first + 1].astype(f32).reshape(size, LANES)
        after = pltpu.roll(after, sub - skip, axis=1)
        tile = jnp.where(lane < sub - skip, tile, after)
        block[k * per_y : (k + 1) * per_y] = tile.reshape(per_y, 8, LANES).astype(block.dtype)
    width = LANES - sub
    lane = lax.broadcasted_iota(jnp.int32, (8, LANES), 1)
    tags = jnp.zeros((8, LANES), f32)
    for s in range(per_y):
        moved = pltpu.roll(got[s, 0].astype(f32), (width * s - sub) % LANES, axis=1)
        tags = jnp.where((lane >= width * s) & (lane < width * (s + 1)), moved, tags)
    block[tiles * per_y] = tags.astype(block.dtype)


def part_kernel(picks, offsets, first, place, *refs):
    *found, gate, up, down, part, weight, rows, spread = refs
    blocks = [found[i] if j is None else found[i].at[j] for i, j in picks]
    f32 = jnp.float32
    lay_rows(place[2], blocks, offsets, first, rows)
    mat = rows[...]
    size = rows.shape[0] // len(blocks)
    per_y = size // 8
    shape = (per_y, 8, LANES)
    lane = lax.broadcasted_iota(jnp.int32, shape, 2)
    want = place[1] + lax.broadcasted_iota(jnp.int32, shape, 0) * (LANES // per_y)
    for block, offset in zip(blocks, offsets):
        tags = jnp.broadcast_to(block[block.shape[0] - 1].astype(f32)[None], shape)
        tags = jnp.sum(jnp.where(lane == want, tags, 0.0), axis=2, keepdims=True)
        base = pl.multiple_of(row_place(place[2], offset, first) * size, size)
        spread[pl.ds(base, size), :] = jnp.broadcast_to(tags, shape).reshape(size, LANES)
    weight[...] = first_fours(spread[...])
    for index, mats in enumerate((gate, up)):
        out = jnp.dot(mat, mats[...], preferred_element_type=f32)
        part[:, index * LANES : (index + 1) * LANES] = first_fours(out).astype(part.dtype)
    out = lax.dot_general(mat, down[...], (((1,), (1,)), ((), ())), preferred_element_type=f32)
    part[:, 2 * LANES :] = last_fours(out).astype(part.dtype)


def grad_kernel(place, *refs):
    *pieces, gate, up, back, wide = refs
    f32, bf16 = jnp.float32, jnp.bfloat16
    quads, weights = pieces[: len(pieces) // 2], pieces[len(pieces) // 2 :]
    sums = []
    for quad in quads:
        total = quad[0].astype(f32)
        for index in range(1, OWNERS):
            total = total + quad[index].astype(f32)
        sums.append(total)
    sums = jnp.concatenate(sums, axis=0)
    weight = jnp.concatenate([w[...] for w in weights], axis=0)
    gate_pre = sums[:, :LANES]
    up_pre = sums[:, LANES : 2 * LANES]
    hidden_grad = sums[:, 2 * LANES :]
    sig = jax.nn.sigmoid(gate_pre)
    hidden = (gate_pre * sig * up_pre).astype(bf16).astype(f32)
    route = jnp.sum(hidden * hidden_grad, axis=1, keepdims=True)
    scaled = weight * hidden_grad
    gate_grad = (scaled * up_pre * sig * (1.0 + gate_pre * (1.0 - sig))).astype(bf16)
    up_grad = (scaled * gate_pre * sig).astype(bf16)
    route_hi, route_lo = hi_lo(route)
    slots = route.shape[0]
    groups, tiles, toks, _ = back.shape
    lane = lax.broadcasted_iota(jnp.int32, (slots, LANES), 1)
    tags = jnp.where(lane == 0, route_hi, jnp.where(lane == 1, route_lo, 0.0))
    count = len(BLOCK_ORDER)
    per_y = groups // count
    homes = [
        pl.multiple_of(lax.rem(place[0] + slot + count, count) * per_y, per_y)
        for slot in BLOCK_ORDER
    ]

    def put(k, tile):
        tile = tile.reshape(groups, toks, LANES).astype(bf16)
        for index, home in enumerate(homes):
            back[pl.ds(home, per_y), k] = tile[index * per_y : (index + 1) * per_y]

    put(tiles - 1, tags)
    across = (((1,), (1,)), ((), ()))
    for k in range(0, tiles - 1, 2):
        cols = slice(k * LANES, (k + 2) * LANES)
        out = lax.dot_general(gate_grad, gate[cols], across, preferred_element_type=f32)
        out = out + lax.dot_general(up_grad, up[cols], across, preferred_element_type=f32)
        for j in range(2):
            put(k + j, out[:, j * LANES : (j + 1) * LANES])
    pairs = slots // 8
    weighted = (weight * hidden).reshape(pairs, 8, LANES)
    mask = upper(weighted.shape)
    even = jnp.where(mask, swap(weighted), 0.0)
    odd = jnp.where(mask, weighted, 0.0)
    wide[...] = jnp.stack([even, odd], axis=1).reshape(pairs * 16, LANES).astype(bf16)


def down_kernel(place, *refs):
    *found, wide, out, rows = refs
    blocks = [found[i] if j is None else found[i].at[j] for i, j in BLOCK_PICKS]
    lay_rows(place[2], blocks, BLOCK_OFFSETS, 0, rows)
    out[...] = lax.dot_general(
        wide[...], rows[...], (((0,), (0,)), ((), ())), preferred_element_type=jnp.float32
    ).astype(out.dtype)


def sum_kernel(sub, landed, pieces, acc):
    f32 = jnp.float32
    experts, owners, tiles, toks, _ = landed.shape
    tags = jnp.zeros((2 * toks, LANES), f32)
    lane = lax.broadcasted_iota(jnp.int32, (toks, LANES), 1)
    tag_hi = jnp.zeros((toks, LANES), f32)
    for e in range(experts):
        pair = landed[e, 0, tiles - 1].astype(f32)
        both = jnp.sum(jnp.where(lane < 2, pair, 0.0), axis=1, keepdims=True)
        tag_hi = jnp.where(lane == sub + e, both, tag_hi)
    tag_hi, tag_lo = hi_lo(tag_hi)
    acc[tiles - 1] = jnp.zeros_like(acc[tiles - 1])
    acc[tiles - 1, :toks] = tag_hi
    acc[tiles - 1, toks : 2 * toks] = tag_lo
    for k in range(tiles - 1):
        for q in range(owners):
            acc[k, q * toks : (q + 1) * toks] = jnp.sum(landed[:, q, k].astype(f32), axis=0)
    tags = acc[tiles - 1]
    lane = lax.broadcasted_iota(jnp.int32, tags.shape, 1)
    for m in range(pieces.shape[0]):
        first, skip = divmod(m * sub, LANES)
        tile = acc[first]
        if skip:
            tile = pltpu.roll(tile, LANES - skip, axis=1)
        if skip + sub > LANES:
            after = pltpu.roll(acc[first + 1], LANES - skip, axis=1)
            tile = jnp.where(lane < LANES - skip, tile, after)
        pieces[m] = jnp.where(lane < sub, tile, tags).astype(pieces.dtype)


def end_kernel(sub, final, ids, token_grad, route_grad, acc):
    f32 = jnp.float32
    toks, owners, _ = token_grad.shape
    acc[...] = jnp.sum(final[...].astype(f32), axis=0)
    for q in range(owners):
        token_grad[:, q, :] = acc[q * toks : (q + 1) * toks, :sub].astype(token_grad.dtype)
    routes = acc[:toks, :] + acc[toks : 2 * toks, :]
    lane = lax.broadcasted_iota(jnp.int32, routes.shape, 1) - sub
    cols = lax.broadcasted_iota(jnp.int32, ids.shape, 1)
    out = jnp.zeros(ids.shape, f32)
    for k in range(ids.shape[1]):
        hit = jnp.sum(jnp.where(lane == ids[:, k : k + 1], routes, 0.0), axis=1, keepdims=True)
        out = jnp.where(cols == k, hit, out)
    route_grad[...] = out


def weight_table(expert_ids, route_weights, experts):
    onehot = expert_ids[:, :, None] == jnp.arange(experts, dtype=jnp.int32)[None, None, :]
    weights = jnp.where(onehot, route_weights.astype(jnp.float32)[:, :, None], 0.0)
    return jnp.sum(weights, axis=1).astype(jnp.bfloat16)


def swap_with(block, toward):
    count = lax.axis_size("y")
    hops = []
    for y in range(count):
        for c in range(2):
            step = 1 if (y + c) % 2 == 0 else -1
            step = step if toward else -step
            hops.append((2 * y + c, 2 * ((y + step) % count) + c))
    return lax.ppermute(block, ("y", "c"), hops)


def body(tokens, out_grad, route_weights, expert_ids, w_gate, w_up, w_down):
    f32, bf16 = jnp.float32, jnp.bfloat16
    ny, nxh, nz = lax.axis_size("y"), lax.axis_size("xh"), lax.axis_size("z")
    experts = ny * nxh
    toks, _, sub = tokens.shape
    per_y = nxh * OWNERS
    groups = ny * per_y
    tall = 2 * toks
    my_y = lax.axis_index("y")
    expert = my_y * nxh + lax.axis_index("xh")
    turn = 1 - 2 * lax.rem(my_y + lax.axis_index("c"), 2)
    place = jnp.stack([my_y, expert, turn]).astype(jnp.int32)

    table = weight_table(expert_ids, route_weights, experts)
    x_rows = jnp.concatenate(
        [tokens.transpose(1, 0, 2), jnp.broadcast_to(table[None], (OWNERS, toks, experts))], axis=2
    )
    g_rows = jnp.pad(out_grad.transpose(1, 0, 2), ((0, 0), (0, 0), (0, LANES - sub)))
    send = jnp.concatenate([x_rows, g_rows], axis=1)
    send = jnp.broadcast_to(send[None, :, None], (nxh, OWNERS, nz, tall, LANES))
    send = send.reshape(nxh * OWNERS * nz, tall, LANES)
    got = lax.all_to_all(send, ("xh", "xl", "c", "z"), 0, 0, tiled=True)
    tiles = nz * sub // LANES
    block = call(
        functools.partial(pack_kernel, sub),
        jax.ShapeDtypeStruct((tiles * per_y + 1, tall, LANES), bf16),
        whole(1),
        [],
        groups * tall * LANES,
        1 << 19,
    )(got.reshape(per_y, nz, tall, LANES))
    smem = pl.BlockSpec(memory_space=pltpu.SMEM)
    slots = groups * toks
    size = per_y * tall
    width = nz * sub

    def partial_sums(found, low, high, first):
        picks = BLOCK_PICKS[low:high]
        used = sorted({i for i, _ in picks})
        local = tuple((used.index(i), j) for i, j in picks)
        n = len(picks)
        part, weight = call(
            functools.partial(part_kernel, local, BLOCK_OFFSETS[low:high], first),
            (
                jax.ShapeDtypeStruct((n * per_y * toks, 3 * LANES), bf16),
                jax.ShapeDtypeStruct((n * per_y * toks, LANES), f32),
            ),
            [smem] + whole(len(used) + 3),
            [pltpu.VMEM((n * size, width), bf16), pltpu.VMEM((n * size, LANES), f32)],
            PART_FLOPS,
            4 << 20,
        )(place, *[found[i] for i in used], w_gate[0], w_up[0], w_down[0])
        return lax.all_gather(part, ("xl", "c"), axis=0, tiled=False), weight

    first = swap_with(block, True)
    other = swap_with(block, False)
    beyond = swap_with(first, False)
    third = swap_with(jnp.stack([other, beyond]), True)
    found = [block, first, other, beyond, third]
    quad_a, weight_a = partial_sums(found, 0, 3, 0)
    third, quad_a = lax.optimization_barrier((third, quad_a))
    found[4] = third
    fourth = swap_with(third, False)
    quad_b, weight_b = partial_sums(found, 3, 5, 3)
    fourth, quad_b = lax.optimization_barrier((fourth, quad_b))
    found.append(fourth)
    quad_c, weight_c = partial_sums(found, 5, 8, 5)

    back, wide = call(
        grad_kernel,
        (
            jax.ShapeDtypeStruct((groups, tiles + 1, toks, LANES), bf16),
            jax.ShapeDtypeStruct((groups * tall, LANES), bf16),
        ),
        [smem] + whole(8),
        [],
        2 * slots * 2 * LANES * nz * LANES,
        3 << 20,
    )(place, quad_a, quad_b, quad_c, weight_a, weight_b, weight_c, w_gate[0], w_up[0])
    landed = lax.all_to_all(back, ("y", "xh", "xl", "c"), 0, 0, tiled=True)

    down_grad = call(
        down_kernel,
        jax.ShapeDtypeStruct((LANES, nz * sub), bf16),
        [smem] + whole(len(found) + 1),
        [pltpu.VMEM((groups * tall, width), bf16)],
        2 * groups * tall * nz * LANES * LANES,
        4 << 20,
    )(place, *found, wide)
    pieces = call(
        functools.partial(sum_kernel, sub),
        jax.ShapeDtypeStruct((nz, OWNERS * toks, LANES), bf16),
        whole(1),
        [pltpu.VMEM((tiles + 1, OWNERS * toks, LANES), f32)],
        groups * toks * nz * LANES,
        1 << 20,
    )(landed.reshape(experts, OWNERS, tiles + 1, toks, LANES))
    final = lax.all_to_all(pieces, "z", 0, 0, tiled=True)
    token_grad, route_grad = call(
        functools.partial(end_kernel, sub),
        (
            jax.ShapeDtypeStruct((toks, OWNERS, sub), bf16),
            jax.ShapeDtypeStruct(expert_ids.shape, f32),
        ),
        whole(2),
        [pltpu.VMEM((OWNERS * toks, LANES), f32)],
        nz * OWNERS * toks * LANES,
        1 << 17,
    )(final, expert_ids)
    return token_grad, down_grad[None], route_grad


def solution(mesh):
    fine = Mesh(
        mesh.devices.reshape(-1, 2, 2, 2, mesh.devices.shape[1]), ("y", "xh", "xl", "c", "z")
    )
    group = ("y", "xh", "xl", "c")
    return jax.shard_map(
        body,
        mesh=fine,
        in_specs=(
            P(group, None, "z"),
            P(group, None, "z"),
            P(group, None),
            P(group, None),
            P(group, None, "z"),
            P(group, None, "z"),
            P(group, "z", None),
        ),
        out_specs=(P(group, None, "z"), P(group, "z", None), P(group, None)),
        check_vma=False,
    )
```

```python
import functools

import jax
import jax.numpy as jnp
from jax import lax
from jax.experimental import pallas as pl
from jax.experimental.pallas import tpu as pltpu
from jax.sharding import Mesh, PartitionSpec as P

OWNERS = 4
LANES = 128


VMEM_LIMIT = 40 * 1024 * 1024
BLOCK_PICKS = ((0, None), (1, None), (2, None), (3, None), (4, 0), (4, 1), (5, 0), (5, 1))
BLOCK_OFFSETS = (0, 1, -1, -2, 2, 3, -3, -4)
BLOCK_ORDER = (0, 1, -1, 2, -2, 3, -3, 4)
PART_FLOPS = 4 * 10**9


def hi_lo(v):
    hi = v.astype(jnp.bfloat16).astype(jnp.float32)
    return hi, v - hi


def call(kernel, out_shape, in_specs, scratch, flops, moved):
    return pl.pallas_call(
        kernel,
        out_shape=out_shape,
        in_specs=in_specs,
        out_specs=jax.tree.map(lambda _: pl.BlockSpec(memory_space=pltpu.VMEM), out_shape),
        scratch_shapes=scratch,
        compiler_params=pltpu.CompilerParams(vmem_limit_bytes=VMEM_LIMIT),
        cost_estimate=pl.CostEstimate(flops=flops, bytes_accessed=moved, transcendentals=0),
    )


def whole(count):
    return [pl.BlockSpec(memory_space=pltpu.VMEM)] * count


def upper(shape):
    return lax.broadcasted_iota(jnp.int32, shape, len(shape) - 2) >= 4


def swap(v):
    return pltpu.roll(v, 4, axis=v.ndim - 2)


def first_fours(v):
    pairs = v.reshape(v.shape[0] // 16, 2, 8, v.shape[1])
    even, odd = pairs[:, 0], pairs[:, 1]
    return jnp.where(upper(even.shape), swap(odd), even).reshape(-1, v.shape[1])


def last_fours(v):
    pairs = v.reshape(v.shape[0] // 16, 2, 8, v.shape[1])
    even, odd = pairs[:, 0], pairs[:, 1]
    return jnp.where(upper(even.shape), odd, swap(even)).reshape(-1, v.shape[1])


def block_offsets(count):
    offsets = [0, 1]
    for step in range(1, count // 2):
        if step % 2:
            offsets += [-step, -step - 1]
        else:
            offsets += [step, step + 1]
    return offsets


def lay_rows(turn, blocks, offsets, first, rows):
    tiles = rows.shape[1] // LANES
    for block, offset in zip(blocks, offsets):
        per_y = block.shape[0] // tiles
        size = per_y * 8
        base = pl.multiple_of(row_place(turn, offset, first) * size, size)
        for k in range(tiles):
            tile = block[k * per_y : (k + 1) * per_y].astype(jnp.float32)
            rows[pl.ds(base, size), k * LANES : (k + 1) * LANES] = tile.reshape(
                size, LANES
            ).astype(jnp.bfloat16)


def row_place(turn, offset, first):
    if offset == 0:
        return 0
    if offset == -4:
        return 7 - first
    ahead = turn if offset > 0 else -turn
    return 2 * abs(offset) - 1 - first + jnp.where(ahead > 0, 0, 1)


def pack_kernel(sub, got, block):
    f32 = jnp.float32
    per_y, nz, _, _ = got.shape
    size = per_y * 8
    tiles = nz * sub // LANES
    lane = lax.broadcasted_iota(jnp.int32, (size, LANES), 1)
    for k in range(tiles):
        first, skip = divmod(k * LANES, sub)
        tile = got[:, first].astype(f32).reshape(size, LANES)
        if skip:
            tile = pltpu.roll(tile, LANES - skip, axis=1)
        after = got[:, first + 1].astype(f32).reshape(size, LANES)
        after = pltpu.roll(after, sub - skip, axis=1)
        tile = jnp.where(lane < sub - skip, tile, after)
        block[k * per_y : (k + 1) * per_y] = tile.reshape(per_y, 8, LANES).astype(block.dtype)
    width = LANES - sub
    lane = lax.broadcasted_iota(jnp.int32, (8, LANES), 1)
    tags = jnp.zeros((8, LANES), f32)
    for s in range(per_y):
        moved = pltpu.roll(got[s, 0].astype(f32), (width * s - sub) % LANES, axis=1)
        tags = jnp.where((lane >= width * s) & (lane < width * (s + 1)), moved, tags)
    block[tiles * per_y] = tags.astype(block.dtype)


def part_kernel(picks, offsets, first, place, *refs):
    *found, gate, up, down, part, weight, rows, spread = refs
    blocks = [found[i] if j is None else found[i].at[j] for i, j in picks]
    f32 = jnp.float32
    lay_rows(place[2], blocks, offsets, first, rows)
    mat = rows[...]
    size = rows.shape[0] // len(blocks)
    per_y = size // 8
    shape = (per_y, 8, LANES)
    lane = lax.broadcasted_iota(jnp.int32, shape, 2)
    want = place[1] + lax.broadcasted_iota(jnp.int32, shape, 0) * (LANES // per_y)
    for block, offset in zip(blocks, offsets):
        tags = jnp.broadcast_to(block[block.shape[0] - 1].astype(f32)[None], shape)
        tags = jnp.sum(jnp.where(lane == want, tags, 0.0), axis=2, keepdims=True)
        base = pl.multiple_of(row_place(place[2], offset, first) * size, size)
        spread[pl.ds(base, size), :] = jnp.broadcast_to(tags, shape).reshape(size, LANES)
    weight[...] = first_fours(spread[...])
    for index, mats in enumerate((gate, up)):
        out = jnp.dot(mat, mats[...], preferred_element_type=f32)
        part[:, index * LANES : (index + 1) * LANES] = first_fours(out).astype(part.dtype)
    out = lax.dot_general(mat, down[...], (((1,), (1,)), ((), ())), preferred_element_type=f32)
    part[:, 2 * LANES :] = last_fours(out).astype(part.dtype)


def grad_kernel(place, *refs):
    *pieces, gate, up, back, wide, moved = refs
    f32, bf16 = jnp.float32, jnp.bfloat16
    quads, weights = pieces[: len(pieces) // 2], pieces[len(pieces) // 2 :]
    sums = []
    for quad in quads:
        total = quad[0].astype(f32)
        for index in range(1, OWNERS):
            total = total + quad[index].astype(f32)
        sums.append(total)
    sums = jnp.concatenate(sums, axis=0)
    weight = jnp.concatenate([w[...] for w in weights], axis=0)
    gate_pre = sums[:, :LANES]
    up_pre = sums[:, LANES : 2 * LANES]
    hidden_grad = sums[:, 2 * LANES :]
    sig = jax.nn.sigmoid(gate_pre)
    hidden = (gate_pre * sig * up_pre).astype(bf16).astype(f32)
    route = jnp.sum(hidden * hidden_grad, axis=1, keepdims=True)
    scaled = weight * hidden_grad
    gate_grad = (scaled * up_pre * sig * (1.0 + gate_pre * (1.0 - sig))).astype(bf16)
    up_grad = (scaled * gate_pre * sig).astype(bf16)
    route_hi, route_lo = hi_lo(route)
    slots = route.shape[0]
    groups, tiles, toks, _ = back.shape
    lane = lax.broadcasted_iota(jnp.int32, (slots, LANES), 1)
    tags = jnp.where(lane == 0, route_hi, jnp.where(lane == 1, route_lo, 0.0))
    count = len(BLOCK_ORDER)
    tall = slots // count
    for index, slot in enumerate(BLOCK_ORDER):
        home = pl.multiple_of(lax.rem(place[0] + slot + count, count) * tall, tall)
        own = slice(index * tall, (index + 1) * tall)
        moved[pl.ds(home, tall), :LANES] = gate_grad[own]
        moved[pl.ds(home, tall), LANES : 2 * LANES] = up_grad[own]
        moved[pl.ds(home, tall), 2 * LANES :] = tags[own].astype(bf16)
    gate_grad, up_grad = moved[:, :LANES], moved[:, LANES : 2 * LANES]

    def put(k, tile):
        back[:, k] = tile.reshape(groups, toks, LANES).astype(bf16)

    put(tiles - 1, moved[:, 2 * LANES :].astype(f32))
    across = (((1,), (1,)), ((), ()))
    for k in range(0, tiles - 1, 2):
        cols = slice(k * LANES, (k + 2) * LANES)
        out = lax.dot_general(gate_grad, gate[cols], across, preferred_element_type=f32)
        out = out + lax.dot_general(up_grad, up[cols], across, preferred_element_type=f32)
        for j in range(2):
            put(k + j, out[:, j * LANES : (j + 1) * LANES])
    pairs = slots // 8
    weighted = (weight * hidden).reshape(pairs, 8, LANES)
    mask = upper(weighted.shape)
    even = jnp.where(mask, swap(weighted), 0.0)
    odd = jnp.where(mask, weighted, 0.0)
    wide[...] = jnp.stack([even, odd], axis=1).reshape(pairs * 16, LANES).astype(bf16)


def down_kernel(place, *refs):
    *found, wide, out, rows = refs
    blocks = [found[i] if j is None else found[i].at[j] for i, j in BLOCK_PICKS]
    lay_rows(place[2], blocks, BLOCK_OFFSETS, 0, rows)
    out[...] = lax.dot_general(
        wide[...], rows[...], (((0,), (0,)), ((), ())), preferred_element_type=jnp.float32
    ).astype(out.dtype)


def sum_kernel(sub, landed, pieces, acc):
    f32 = jnp.float32
    experts, owners, tiles, toks, _ = landed.shape
    tags = jnp.zeros((2 * toks, LANES), f32)
    lane = lax.broadcasted_iota(jnp.int32, (toks, LANES), 1)
    tag_hi = jnp.zeros((toks, LANES), f32)
    for e in range(experts):
        pair = landed[e, 0, tiles - 1].astype(f32)
        both = jnp.sum(jnp.where(lane < 2, pair, 0.0), axis=1, keepdims=True)
        tag_hi = jnp.where(lane == sub + e, both, tag_hi)
    tag_hi, tag_lo = hi_lo(tag_hi)
    acc[tiles - 1] = jnp.zeros_like(acc[tiles - 1])
    acc[tiles - 1, :toks] = tag_hi
    acc[tiles - 1, toks : 2 * toks] = tag_lo
    for k in range(tiles - 1):
        for q in range(owners):
            acc[k, q * toks : (q + 1) * toks] = jnp.sum(landed[:, q, k].astype(f32), axis=0)
    tags = acc[tiles - 1]
    lane = lax.broadcasted_iota(jnp.int32, tags.shape, 1)
    for m in range(pieces.shape[0]):
        first, skip = divmod(m * sub, LANES)
        tile = acc[first]
        if skip:
            tile = pltpu.roll(tile, LANES - skip, axis=1)
        if skip + sub > LANES:
            after = pltpu.roll(acc[first + 1], LANES - skip, axis=1)
            tile = jnp.where(lane < LANES - skip, tile, after)
        pieces[m] = jnp.where(lane < sub, tile, tags).astype(pieces.dtype)


def end_kernel(sub, final, ids, token_grad, route_grad, acc):
    f32 = jnp.float32
    toks, owners, _ = token_grad.shape
    acc[...] = jnp.sum(final[...].astype(f32), axis=0)
    for q in range(owners):
        token_grad[:, q, :] = acc[q * toks : (q + 1) * toks, :sub].astype(token_grad.dtype)
    routes = acc[:toks, :] + acc[toks : 2 * toks, :]
    lane = lax.broadcasted_iota(jnp.int32, routes.shape, 1) - sub
    cols = lax.broadcasted_iota(jnp.int32, ids.shape, 1)
    out = jnp.zeros(ids.shape, f32)
    for k in range(ids.shape[1]):
        hit = jnp.sum(jnp.where(lane == ids[:, k : k + 1], routes, 0.0), axis=1, keepdims=True)
        out = jnp.where(cols == k, hit, out)
    route_grad[...] = out


def send_kernel(tokens, out_grad, weights, ids, send, acc):
    f32 = jnp.float32
    toks, owners, sub = tokens.shape
    x_rows = tokens[...].astype(f32)
    g_rows = out_grad[...].astype(f32)
    acc[...] = jnp.zeros_like(acc)
    for q in range(owners):
        acc[q, :toks, :sub] = x_rows[:, q, :]
        acc[q, toks : 2 * toks, :sub] = g_rows[:, q, :]
    route = weights[...].astype(f32)
    lane = lax.broadcasted_iota(jnp.int32, (toks, LANES), 1) - sub
    table = jnp.zeros((toks, LANES), f32)
    for k in range(ids.shape[1]):
        table = jnp.where(lane == ids[:, k : k + 1], route[:, k : k + 1], table)
    acc[owners, :toks, :] = table
    for q in range(owners):
        tile = (acc[q] + acc[owners]).astype(send.dtype)
        for top in range(q, send.shape[0], owners):
            send[top] = jnp.broadcast_to(tile[None], send.shape[1:])


def swap_with(block, toward):
    count = lax.axis_size("y")
    hops = []
    for y in range(count):
        for c in range(2):
            step = 1 if (y + c) % 2 == 0 else -1
            step = step if toward else -step
            hops.append((2 * y + c, 2 * ((y + step) % count) + c))
    return lax.ppermute(block, ("y", "c"), hops)


def body(tokens, out_grad, route_weights, expert_ids, w_gate, w_up, w_down):
    f32, bf16 = jnp.float32, jnp.bfloat16
    ny, nxh, nz = lax.axis_size("y"), lax.axis_size("xh"), lax.axis_size("z")
    experts = ny * nxh
    toks, _, sub = tokens.shape
    per_y = nxh * OWNERS
    groups = ny * per_y
    tall = 2 * toks
    my_y = lax.axis_index("y")
    expert = my_y * nxh + lax.axis_index("xh")
    turn = 1 - 2 * lax.rem(my_y + lax.axis_index("c"), 2)
    place = jnp.stack([my_y, expert, turn]).astype(jnp.int32)

    send = call(
        send_kernel,
        jax.ShapeDtypeStruct((nxh * OWNERS, nz, tall, LANES), bf16),
        whole(4),
        [pltpu.VMEM((OWNERS + 1, tall, LANES), f32)],
        per_y * nz * tall * LANES,
        1 << 19,
    )(tokens, out_grad, route_weights, expert_ids)
    send = send.reshape(nxh * OWNERS * nz, tall, LANES)
    got = lax.all_to_all(send, ("xh", "xl", "c", "z"), 0, 0, tiled=True)
    tiles = nz * sub // LANES
    block = call(
        functools.partial(pack_kernel, sub),
        jax.ShapeDtypeStruct((tiles * per_y + 1, tall, LANES), bf16),
        whole(1),
        [],
        groups * tall * LANES,
        1 << 19,
    )(got.reshape(per_y, nz, tall, LANES))
    smem = pl.BlockSpec(memory_space=pltpu.SMEM)
    slots = groups * toks
    size = per_y * tall
    width = nz * sub

    def partial_sums(found, low, high, first):
        picks = BLOCK_PICKS[low:high]
        used = sorted({i for i, _ in picks})
        local = tuple((used.index(i), j) for i, j in picks)
        n = len(picks)
        part, weight = call(
            functools.partial(part_kernel, local, BLOCK_OFFSETS[low:high], first),
            (
                jax.ShapeDtypeStruct((n * per_y * toks, 3 * LANES), bf16),
                jax.ShapeDtypeStruct((n * per_y * toks, LANES), f32),
            ),
            [smem] + whole(len(used) + 3),
            [pltpu.VMEM((n * size, width), bf16), pltpu.VMEM((n * size, LANES), f32)],
            PART_FLOPS,
            4 << 20,
        )(place, *[found[i] for i in used], w_gate[0], w_up[0], w_down[0])
        return lax.all_gather(part, ("xl", "c"), axis=0, tiled=False), weight

    first = swap_with(block, True)
    other = swap_with(block, False)
    beyond = swap_with(first, False)
    third = swap_with(jnp.stack([other, beyond]), True)
    found = [block, first, other, beyond, third]
    quad_a, weight_a = partial_sums(found, 0, 3, 0)
    third, quad_a = lax.optimization_barrier((third, quad_a))
    found[4] = third
    fourth = swap_with(third, False)
    quad_b, weight_b = partial_sums(found, 3, 5, 3)
    fourth, quad_b = lax.optimization_barrier((fourth, quad_b))
    found.append(fourth)
    quad_c, weight_c = partial_sums(found, 5, 8, 5)

    back, wide = call(
        grad_kernel,
        (
            jax.ShapeDtypeStruct((groups, tiles + 1, toks, LANES), bf16),
            jax.ShapeDtypeStruct((groups * tall, LANES), bf16),
        ),
        [smem] + whole(8),
        [pltpu.VMEM((slots, 3 * LANES), bf16)],
        2 * slots * 2 * LANES * nz * LANES,
        3 << 20,
    )(place, quad_a, quad_b, quad_c, weight_a, weight_b, weight_c, w_gate[0], w_up[0])
    landed = lax.all_to_all(back, ("y", "xh", "xl", "c"), 0, 0, tiled=True)

    down_grad = call(
        down_kernel,
        jax.ShapeDtypeStruct((LANES, nz * sub), bf16),
        [smem] + whole(len(found) + 1),
        [pltpu.VMEM((groups * tall, width), bf16)],
        2 * groups * tall * nz * LANES * LANES,
        4 << 20,
    )(place, *found, wide)
    pieces = call(
        functools.partial(sum_kernel, sub),
        jax.ShapeDtypeStruct((nz, OWNERS * toks, LANES), bf16),
        whole(1),
        [pltpu.VMEM((tiles + 1, OWNERS * toks, LANES), f32)],
        groups * toks * nz * LANES,
        1 << 20,
    )(landed.reshape(experts, OWNERS, tiles + 1, toks, LANES))
    final = lax.all_to_all(pieces, "z", 0, 0, tiled=True)
    token_grad, route_grad = call(
        functools.partial(end_kernel, sub),
        (
            jax.ShapeDtypeStruct((toks, OWNERS, sub), bf16),
            jax.ShapeDtypeStruct(expert_ids.shape, f32),
        ),
        whole(2),
        [pltpu.VMEM((OWNERS * toks, LANES), f32)],
        nz * OWNERS * toks * LANES,
        1 << 17,
    )(final, expert_ids)
    return token_grad, down_grad[None], route_grad


def solution(mesh):
    fine = Mesh(
        mesh.devices.reshape(-1, 2, 2, 2, mesh.devices.shape[1]), ("y", "xh", "xl", "c", "z")
    )
    group = ("y", "xh", "xl", "c")
    return jax.shard_map(
        body,
        mesh=fine,
        in_specs=(
            P(group, None, "z"),
            P(group, None, "z"),
            P(group, None),
            P(group, None),
            P(group, None, "z"),
            P(group, None, "z"),
            P(group, "z", None),
        ),
        out_specs=(P(group, None, "z"), P(group, "z", None), P(group, None)),
        check_vma=False,
    )
```

```python
import functools

import jax
import jax.numpy as jnp
from jax import lax
from jax.experimental import pallas as pl
from jax.experimental.pallas import tpu as pltpu
from jax.sharding import Mesh, PartitionSpec as P

OWNERS = 4
LANES = 128


VMEM_LIMIT = 40 * 1024 * 1024
BLOCK_PICKS = ((0, None), (1, None), (2, None), (3, None), (4, 0), (4, 1), (5, 0), (5, 1))
BLOCK_OFFSETS = (0, 1, -1, -2, 2, 3, -3, -4)
BLOCK_ORDER = (0, 1, -1, 2, -2, 3, -3, 4)
PART_FLOPS = 4 * 10**9


def hi_lo(v):
    hi = v.astype(jnp.bfloat16).astype(jnp.float32)
    return hi, v - hi


def call(kernel, out_shape, in_specs, scratch, flops, moved):
    return pl.pallas_call(
        kernel,
        out_shape=out_shape,
        in_specs=in_specs,
        out_specs=jax.tree.map(lambda _: pl.BlockSpec(memory_space=pltpu.VMEM), out_shape),
        scratch_shapes=scratch,
        compiler_params=pltpu.CompilerParams(vmem_limit_bytes=VMEM_LIMIT),
        cost_estimate=pl.CostEstimate(flops=flops, bytes_accessed=moved, transcendentals=0),
    )


def whole(count):
    return [pl.BlockSpec(memory_space=pltpu.VMEM)] * count


def upper(shape):
    return lax.broadcasted_iota(jnp.int32, shape, len(shape) - 2) >= 4


def swap(v):
    return pltpu.roll(v, 4, axis=v.ndim - 2)


def first_fours(v):
    pairs = v.reshape(v.shape[0] // 16, 2, 8, v.shape[1])
    even, odd = pairs[:, 0], pairs[:, 1]
    return jnp.where(upper(even.shape), swap(odd), even).reshape(-1, v.shape[1])


def last_fours(v):
    pairs = v.reshape(v.shape[0] // 16, 2, 8, v.shape[1])
    even, odd = pairs[:, 0], pairs[:, 1]
    return jnp.where(upper(even.shape), odd, swap(even)).reshape(-1, v.shape[1])


def block_offsets(count):
    offsets = [0, 1]
    for step in range(1, count // 2):
        if step % 2:
            offsets += [-step, -step - 1]
        else:
            offsets += [step, step + 1]
    return offsets


def lay_rows(turn, blocks, offsets, first, rows):
    tiles = rows.shape[1] // LANES
    for block, offset in zip(blocks, offsets):
        per_y = block.shape[0] // tiles
        size = per_y * 8
        base = pl.multiple_of(row_place(turn, offset, first) * size, size)
        for k in range(tiles):
            tile = block[k * per_y : (k + 1) * per_y].astype(jnp.float32)
            rows[pl.ds(base, size), k * LANES : (k + 1) * LANES] = tile.reshape(
                size, LANES
            ).astype(jnp.bfloat16)


def row_place(turn, offset, first):
    if offset == 0:
        return 0
    if offset == -4:
        return 7 - first
    ahead = turn if offset > 0 else -turn
    return 2 * abs(offset) - 1 - first + jnp.where(ahead > 0, 0, 1)


def pack_kernel(sub, got, block):
    f32 = jnp.float32
    per_y, nz, _, _ = got.shape
    size = per_y * 8
    tiles = nz * sub // LANES
    lane = lax.broadcasted_iota(jnp.int32, (size, LANES), 1)
    for k in range(tiles):
        first, skip = divmod(k * LANES, sub)
        tile = got[:, first].astype(f32).reshape(size, LANES)
        if skip:
            tile = pltpu.roll(tile, LANES - skip, axis=1)
        after = got[:, first + 1].astype(f32).reshape(size, LANES)
        after = pltpu.roll(after, sub - skip, axis=1)
        tile = jnp.where(lane < sub - skip, tile, after)
        block[k * per_y : (k + 1) * per_y] = tile.reshape(per_y, 8, LANES).astype(block.dtype)
    width = LANES - sub
    lane = lax.broadcasted_iota(jnp.int32, (8, LANES), 1)
    tags = jnp.zeros((8, LANES), f32)
    for s in range(per_y):
        moved = pltpu.roll(got[s, 0].astype(f32), (width * s - sub) % LANES, axis=1)
        tags = jnp.where((lane >= width * s) & (lane < width * (s + 1)), moved, tags)
    block[tiles * per_y] = tags.astype(block.dtype)


def position():
    my_y = lax.axis_index("y")
    expert = my_y * lax.axis_size("xh") + lax.axis_index("xh")
    return my_y, expert, 1 - 2 * lax.rem(my_y + lax.axis_index("c"), 2)


def part_kernel(picks, offsets, first, *refs):
    place = position()
    *found, gate, up, down, part, weight, rows, spread = refs
    blocks = [found[i] if j is None else found[i].at[j] for i, j in picks]
    f32 = jnp.float32
    lay_rows(place[2], blocks, offsets, first, rows)
    mat = rows[...]
    size = rows.shape[0] // len(blocks)
    per_y = size // 8
    shape = (per_y, 8, LANES)
    lane = lax.broadcasted_iota(jnp.int32, shape, 2)
    want = place[1] + lax.broadcasted_iota(jnp.int32, shape, 0) * (LANES // per_y)
    for block, offset in zip(blocks, offsets):
        tags = jnp.broadcast_to(block[block.shape[0] - 1].astype(f32)[None], shape)
        tags = jnp.sum(jnp.where(lane == want, tags, 0.0), axis=2, keepdims=True)
        base = pl.multiple_of(row_place(place[2], offset, first) * size, size)
        spread[pl.ds(base, size), :] = jnp.broadcast_to(tags, shape).reshape(size, LANES)
    weight[...] = first_fours(spread[...])
    for index, mats in enumerate((gate, up)):
        out = jnp.dot(mat, mats[...], preferred_element_type=f32)
        part[:, index * LANES : (index + 1) * LANES] = first_fours(out).astype(part.dtype)
    out = lax.dot_general(mat, down[...], (((1,), (1,)), ((), ())), preferred_element_type=f32)
    part[:, 2 * LANES :] = last_fours(out).astype(part.dtype)


def grad_kernel(*refs):
    place = position()
    *pieces, gate, up, back, wide, moved = refs
    f32, bf16 = jnp.float32, jnp.bfloat16
    quads, weights = pieces[: len(pieces) // 2], pieces[len(pieces) // 2 :]
    sums = []
    for quad in quads:
        total = quad[0].astype(f32)
        for index in range(1, OWNERS):
            total = total + quad[index].astype(f32)
        sums.append(total)
    sums = jnp.concatenate(sums, axis=0)
    weight = jnp.concatenate([w[...] for w in weights], axis=0)
    gate_pre = sums[:, :LANES]
    up_pre = sums[:, LANES : 2 * LANES]
    hidden_grad = sums[:, 2 * LANES :]
    sig = jax.nn.sigmoid(gate_pre)
    hidden = (gate_pre * sig * up_pre).astype(bf16).astype(f32)
    route = jnp.sum(hidden * hidden_grad, axis=1, keepdims=True)
    scaled = weight * hidden_grad
    gate_grad = (scaled * up_pre * sig * (1.0 + gate_pre * (1.0 - sig))).astype(bf16)
    up_grad = (scaled * gate_pre * sig).astype(bf16)
    route_hi, route_lo = hi_lo(route)
    slots = route.shape[0]
    groups, tiles, toks, _ = back.shape
    lane = lax.broadcasted_iota(jnp.int32, (slots, LANES), 1)
    tags = jnp.where(lane == 0, route_hi, jnp.where(lane == 1, route_lo, 0.0))
    count = len(BLOCK_ORDER)
    tall = slots // count
    for index, slot in enumerate(BLOCK_ORDER):
        home = pl.multiple_of(lax.rem(place[0] + slot + count, count) * tall, tall)
        own = slice(index * tall, (index + 1) * tall)
        moved[pl.ds(home, tall), :LANES] = gate_grad[own]
        moved[pl.ds(home, tall), LANES : 2 * LANES] = up_grad[own]
        moved[pl.ds(home, tall), 2 * LANES :] = tags[own].astype(bf16)
    gate_grad, up_grad = moved[:, :LANES], moved[:, LANES : 2 * LANES]

    def put(k, tile):
        back[:, k] = tile.reshape(groups, toks, LANES).astype(bf16)

    put(tiles - 1, moved[:, 2 * LANES :].astype(f32))
    across = (((1,), (1,)), ((), ()))
    for k in range(0, tiles - 1, 2):
        cols = slice(k * LANES, (k + 2) * LANES)
        out = lax.dot_general(gate_grad, gate[cols], across, preferred_element_type=f32)
        out = out + lax.dot_general(up_grad, up[cols], across, preferred_element_type=f32)
        for j in range(2):
            put(k + j, out[:, j * LANES : (j + 1) * LANES])
    pairs = slots // 8
    weighted = (weight * hidden).reshape(pairs, 8, LANES)
    mask = upper(weighted.shape)
    even = jnp.where(mask, swap(weighted), 0.0)
    odd = jnp.where(mask, weighted, 0.0)
    wide[...] = jnp.stack([even, odd], axis=1).reshape(pairs * 16, LANES).astype(bf16)


def down_kernel(*refs):
    place = position()
    *found, wide, out, rows = refs
    blocks = [found[i] if j is None else found[i].at[j] for i, j in BLOCK_PICKS]
    lay_rows(place[2], blocks, BLOCK_OFFSETS, 0, rows)
    out[...] = lax.dot_general(
        wide[...], rows[...], (((0,), (0,)), ((), ())), preferred_element_type=jnp.float32
    ).astype(out.dtype)


def sum_kernel(sub, landed, pieces, acc):
    f32 = jnp.float32
    experts, owners, tiles, toks, _ = landed.shape
    tags = jnp.zeros((2 * toks, LANES), f32)
    lane = lax.broadcasted_iota(jnp.int32, (toks, LANES), 1)
    tag_hi = jnp.zeros((toks, LANES), f32)
    for e in range(experts):
        pair = landed[e, 0, tiles - 1].astype(f32)
        both = jnp.sum(jnp.where(lane < 2, pair, 0.0), axis=1, keepdims=True)
        tag_hi = jnp.where(lane == sub + e, both, tag_hi)
    tag_hi, tag_lo = hi_lo(tag_hi)
    acc[tiles - 1] = jnp.zeros_like(acc[tiles - 1])
    acc[tiles - 1, :toks] = tag_hi
    acc[tiles - 1, toks : 2 * toks] = tag_lo
    for k in range(tiles - 1):
        for q in range(owners):
            acc[k, q * toks : (q + 1) * toks] = jnp.sum(landed[:, q, k].astype(f32), axis=0)
    tags = acc[tiles - 1]
    lane = lax.broadcasted_iota(jnp.int32, tags.shape, 1)
    for m in range(pieces.shape[0]):
        first, skip = divmod(m * sub, LANES)
        tile = acc[first]
        if skip:
            tile = pltpu.roll(tile, LANES - skip, axis=1)
        if skip + sub > LANES:
            after = pltpu.roll(acc[first + 1], LANES - skip, axis=1)
            tile = jnp.where(lane < LANES - skip, tile, after)
        pieces[m] = jnp.where(lane < sub, tile, tags).astype(pieces.dtype)


def end_kernel(sub, final, ids, token_grad, route_grad, acc):
    f32 = jnp.float32
    toks, owners, _ = token_grad.shape
    acc[...] = jnp.sum(final[...].astype(f32), axis=0)
    for q in range(owners):
        token_grad[:, q, :] = acc[q * toks : (q + 1) * toks, :sub].astype(token_grad.dtype)
    routes = acc[:toks, :] + acc[toks : 2 * toks, :]
    lane = lax.broadcasted_iota(jnp.int32, routes.shape, 1) - sub
    cols = lax.broadcasted_iota(jnp.int32, ids.shape, 1)
    out = jnp.zeros(ids.shape, f32)
    for k in range(ids.shape[1]):
        hit = jnp.sum(jnp.where(lane == ids[:, k : k + 1], routes, 0.0), axis=1, keepdims=True)
        out = jnp.where(cols == k, hit, out)
    route_grad[...] = out


def send_kernel(*refs):
    f32 = jnp.float32
    far, send, acc, near, sems = refs[:4], refs[4], refs[5], refs[6:10], refs[10]
    copies = [pltpu.make_async_copy(a, b, sems.at[i]) for i, (a, b) in enumerate(zip(far, near))]
    for copy in copies:
        copy.start()
    for copy in copies:
        copy.wait()
    tokens, out_grad, weights, ids = near
    toks, owners, sub = tokens.shape
    x_rows = tokens[...].astype(f32)
    g_rows = out_grad[...].astype(f32)
    acc[...] = jnp.zeros_like(acc)
    for q in range(owners):
        acc[q, :toks, :sub] = x_rows[:, q, :]
        acc[q, toks : 2 * toks, :sub] = g_rows[:, q, :]
    route = weights[...].astype(f32)
    lane = lax.broadcasted_iota(jnp.int32, (toks, LANES), 1) - sub
    table = jnp.zeros((toks, LANES), f32)
    for k in range(ids.shape[1]):
        table = jnp.where(lane == ids[:, k : k + 1], route[:, k : k + 1], table)
    acc[owners, :toks, :] = table
    for q in range(owners):
        tile = (acc[q] + acc[owners]).astype(send.dtype)
        for top in range(q, send.shape[0], owners):
            send[top] = jnp.broadcast_to(tile[None], send.shape[1:])


def swap_with(block, toward):
    count = lax.axis_size("y")
    hops = []
    for y in range(count):
        for c in range(2):
            step = 1 if (y + c) % 2 == 0 else -1
            step = step if toward else -step
            hops.append((2 * y + c, 2 * ((y + step) % count) + c))
    return lax.ppermute(block, ("y", "c"), hops)


def body(tokens, out_grad, route_weights, expert_ids, w_gate, w_up, w_down):
    f32, bf16 = jnp.float32, jnp.bfloat16
    ny, nxh, nz = lax.axis_size("y"), lax.axis_size("xh"), lax.axis_size("z")
    experts = ny * nxh
    toks, _, sub = tokens.shape
    per_y = nxh * OWNERS
    groups = ny * per_y
    tall = 2 * toks
    send = call(
        send_kernel,
        jax.ShapeDtypeStruct((nxh * OWNERS, nz, tall, LANES), bf16),
        [pl.BlockSpec(memory_space=pltpu.HBM)] * 4,
        [
            pltpu.VMEM((OWNERS + 1, tall, LANES), f32),
            pltpu.VMEM(tokens.shape, bf16),
            pltpu.VMEM(out_grad.shape, bf16),
            pltpu.VMEM(route_weights.shape, bf16),
            pltpu.VMEM(expert_ids.shape, jnp.int32),
            pltpu.SemaphoreType.DMA((4,)),
        ],
        per_y * nz * tall * LANES,
        1 << 19,
    )(tokens, out_grad, route_weights, expert_ids)
    send = send.reshape(nxh * OWNERS * nz, tall, LANES)
    got = lax.all_to_all(send, ("xh", "xl", "c", "z"), 0, 0, tiled=True)
    tiles = nz * sub // LANES
    block = call(
        functools.partial(pack_kernel, sub),
        jax.ShapeDtypeStruct((tiles * per_y + 1, tall, LANES), bf16),
        whole(1),
        [],
        groups * tall * LANES,
        1 << 19,
    )(got.reshape(per_y, nz, tall, LANES))
    slots = groups * toks
    size = per_y * tall
    width = nz * sub

    def partial_sums(found, low, high, first):
        picks = BLOCK_PICKS[low:high]
        used = sorted({i for i, _ in picks})
        local = tuple((used.index(i), j) for i, j in picks)
        n = len(picks)
        part, weight = call(
            functools.partial(part_kernel, local, BLOCK_OFFSETS[low:high], first),
            (
                jax.ShapeDtypeStruct((n * per_y * toks, 3 * LANES), bf16),
                jax.ShapeDtypeStruct((n * per_y * toks, LANES), f32),
            ),
            whole(len(used) + 3),
            [pltpu.VMEM((n * size, width), bf16), pltpu.VMEM((n * size, LANES), f32)],
            PART_FLOPS,
            4 << 20,
        )(*[found[i] for i in used], w_gate[0], w_up[0], w_down[0])
        return lax.all_gather(part, ("xl", "c"), axis=0, tiled=False), weight

    first = swap_with(block, True)
    other = swap_with(block, False)
    beyond = swap_with(first, False)
    third = swap_with(jnp.stack([other, beyond]), True)
    found = [block, first, other, beyond, third]
    quad_a, weight_a = partial_sums(found, 0, 3, 0)
    third, quad_a = lax.optimization_barrier((third, quad_a))
    found[4] = third
    fourth = swap_with(third, False)
    quad_b, weight_b = partial_sums(found, 3, 5, 3)
    fourth, quad_b = lax.optimization_barrier((fourth, quad_b))
    found.append(fourth)
    quad_c, weight_c = partial_sums(found, 5, 8, 5)

    back, wide = call(
        grad_kernel,
        (
            jax.ShapeDtypeStruct((groups, tiles + 1, toks, LANES), bf16),
            jax.ShapeDtypeStruct((groups * tall, LANES), bf16),
        ),
        whole(8),
        [pltpu.VMEM((slots, 3 * LANES), bf16)],
        2 * slots * 2 * LANES * nz * LANES,
        3 << 20,
    )(quad_a, quad_b, quad_c, weight_a, weight_b, weight_c, w_gate[0], w_up[0])
    landed = lax.all_to_all(back, ("y", "xh", "xl", "c"), 0, 0, tiled=True)

    down_grad = call(
        down_kernel,
        jax.ShapeDtypeStruct((LANES, nz * sub), bf16),
        whole(len(found) + 1),
        [pltpu.VMEM((groups * tall, width), bf16)],
        2 * groups * tall * nz * LANES * LANES,
        4 << 20,
    )(*found, wide)
    pieces = call(
        functools.partial(sum_kernel, sub),
        jax.ShapeDtypeStruct((nz, OWNERS * toks, LANES), bf16),
        whole(1),
        [pltpu.VMEM((tiles + 1, OWNERS * toks, LANES), f32)],
        groups * toks * nz * LANES,
        1 << 20,
    )(landed.reshape(experts, OWNERS, tiles + 1, toks, LANES))
    final = lax.all_to_all(pieces, "z", 0, 0, tiled=True)
    token_grad, route_grad = call(
        functools.partial(end_kernel, sub),
        (
            jax.ShapeDtypeStruct((toks, OWNERS, sub), bf16),
            jax.ShapeDtypeStruct(expert_ids.shape, f32),
        ),
        whole(2),
        [pltpu.VMEM((OWNERS * toks, LANES), f32)],
        nz * OWNERS * toks * LANES,
        1 << 17,
    )(final, expert_ids)
    return token_grad, down_grad[None], route_grad


def solution(mesh):
    fine = Mesh(
        mesh.devices.reshape(-1, 2, 2, 2, mesh.devices.shape[1]), ("y", "xh", "xl", "c", "z")
    )
    group = ("y", "xh", "xl", "c")
    return jax.shard_map(
        body,
        mesh=fine,
        in_specs=(
            P(group, None, "z"),
            P(group, None, "z"),
            P(group, None),
            P(group, None),
            P(group, None, "z"),
            P(group, None, "z"),
            P(group, "z", None),
        ),
        out_specs=(P(group, None, "z"), P(group, "z", None), P(group, None)),
        check_vma=False,
    )
```

```python
import functools

import jax
import jax.numpy as jnp
from jax import lax
from jax.experimental import pallas as pl
from jax.experimental.pallas import tpu as pltpu
from jax.sharding import Mesh, PartitionSpec as P

OWNERS = 4
LANES = 128


VMEM_LIMIT = 40 * 1024 * 1024
BLOCK_PICKS = ((0, None), (1, None), (2, None), (3, None), (4, 0), (4, 1), (5, 0), (5, 1))
BLOCK_OFFSETS = (0, 1, -1, -2, 2, 3, -3, -4)
BLOCK_ORDER = (0, 1, -1, 2, -2, 3, -3, 4)
PART_FLOPS = 4 * 10**9


def hi_lo(v):
    hi = v.astype(jnp.bfloat16).astype(jnp.float32)
    return hi, v - hi


def call(kernel, out_shape, in_specs, scratch, flops, moved):
    return pl.pallas_call(
        kernel,
        out_shape=out_shape,
        in_specs=in_specs,
        out_specs=jax.tree.map(lambda _: pl.BlockSpec(memory_space=pltpu.VMEM), out_shape),
        scratch_shapes=scratch,
        compiler_params=pltpu.CompilerParams(vmem_limit_bytes=VMEM_LIMIT),
        cost_estimate=pl.CostEstimate(flops=flops, bytes_accessed=moved, transcendentals=0),
    )


def whole(count):
    return [pl.BlockSpec(memory_space=pltpu.VMEM)] * count


def upper(shape):
    return lax.broadcasted_iota(jnp.int32, shape, len(shape) - 2) >= 4


def swap(v):
    return pltpu.roll(v, 4, axis=v.ndim - 2)


def first_fours(v):
    pairs = v.reshape(v.shape[0] // 16, 2, 8, v.shape[1])
    even, odd = pairs[:, 0], pairs[:, 1]
    return jnp.where(upper(even.shape), swap(odd), even).reshape(-1, v.shape[1])


def last_fours(v):
    pairs = v.reshape(v.shape[0] // 16, 2, 8, v.shape[1])
    even, odd = pairs[:, 0], pairs[:, 1]
    return jnp.where(upper(even.shape), odd, swap(even)).reshape(-1, v.shape[1])


def block_offsets(count):
    offsets = [0, 1]
    for step in range(1, count // 2):
        if step % 2:
            offsets += [-step, -step - 1]
        else:
            offsets += [step, step + 1]
    return offsets


def lay_rows(turn, blocks, offsets, first, rows):
    tiles = rows.shape[1] // LANES
    for block, offset in zip(blocks, offsets):
        per_y = block.shape[0] // tiles
        size = per_y * 8
        base = pl.multiple_of(row_place(turn, offset, first) * size, size)
        for k in range(tiles):
            tile = block[k * per_y : (k + 1) * per_y].astype(jnp.float32)
            rows[pl.ds(base, size), k * LANES : (k + 1) * LANES] = tile.reshape(
                size, LANES
            ).astype(jnp.bfloat16)


def row_place(turn, offset, first):
    if offset == 0:
        return 0
    if offset == -4:
        return 7 - first
    ahead = turn if offset > 0 else -turn
    return 2 * abs(offset) - 1 - first + jnp.where(ahead > 0, 0, 1)


def pack_kernel(sub, got, block):
    f32 = jnp.float32
    per_y, nz, _, _ = got.shape
    size = per_y * 8
    tiles = nz * sub // LANES
    lane = lax.broadcasted_iota(jnp.int32, (size, LANES), 1)
    for k in range(tiles):
        first, skip = divmod(k * LANES, sub)
        tile = got[:, first].astype(f32).reshape(size, LANES)
        if skip:
            tile = pltpu.roll(tile, LANES - skip, axis=1)
        after = got[:, first + 1].astype(f32).reshape(size, LANES)
        after = pltpu.roll(after, sub - skip, axis=1)
        tile = jnp.where(lane < sub - skip, tile, after)
        block[k * per_y : (k + 1) * per_y] = tile.reshape(per_y, 8, LANES).astype(block.dtype)
    width = LANES - sub
    lane = lax.broadcasted_iota(jnp.int32, (8, LANES), 1)
    tags = jnp.zeros((8, LANES), f32)
    for s in range(per_y):
        moved = pltpu.roll(got[s, 0].astype(f32), (width * s - sub) % LANES, axis=1)
        tags = jnp.where((lane >= width * s) & (lane < width * (s + 1)), moved, tags)
    block[tiles * per_y] = tags.astype(block.dtype)


def position():
    my_y = lax.axis_index("y")
    expert = my_y * lax.axis_size("xh") + lax.axis_index("xh")
    return my_y, expert, 1 - 2 * lax.rem(my_y + lax.axis_index("c"), 2)


def part_kernel(picks, offsets, first, *refs):
    place = position()
    *found, gate, up, down, part, weight, rows, spread = refs
    blocks = [found[i] if j is None else found[i].at[j] for i, j in picks]
    f32 = jnp.float32
    lay_rows(place[2], blocks, offsets, first, rows)
    mat = rows[...]
    size = rows.shape[0] // len(blocks)
    per_y = size // 8
    shape = (per_y, 8, LANES)
    lane = lax.broadcasted_iota(jnp.int32, shape, 2)
    want = place[1] + lax.broadcasted_iota(jnp.int32, shape, 0) * (LANES // per_y)
    for block, offset in zip(blocks, offsets):
        tags = jnp.broadcast_to(block[block.shape[0] - 1].astype(f32)[None], shape)
        tags = jnp.sum(jnp.where(lane == want, tags, 0.0), axis=2, keepdims=True)
        base = pl.multiple_of(row_place(place[2], offset, first) * size, size)
        spread[pl.ds(base, size), :] = jnp.broadcast_to(tags, shape).reshape(size, LANES)
    weight[...] = first_fours(spread[...])
    for index, mats in enumerate((gate, up)):
        out = jnp.dot(mat, mats[...], preferred_element_type=f32)
        part[:, index * LANES : (index + 1) * LANES] = first_fours(out).astype(part.dtype)
    out = lax.dot_general(mat, down[...], (((1,), (1,)), ((), ())), preferred_element_type=f32)
    part[:, 2 * LANES :] = last_fours(out).astype(part.dtype)


def grad_kernel(*refs):
    place = position()
    *pieces, gate, up, back, wide, moved = refs
    f32, bf16 = jnp.float32, jnp.bfloat16
    quads, weights = pieces[: len(pieces) // 2], pieces[len(pieces) // 2 :]
    sums = []
    for quad in quads:
        total = quad[0].astype(f32)
        for index in range(1, OWNERS):
            total = total + quad[index].astype(f32)
        sums.append(total)
    sums = jnp.concatenate(sums, axis=0)
    weight = jnp.concatenate([w[...] for w in weights], axis=0)
    gate_pre = sums[:, :LANES]
    up_pre = sums[:, LANES : 2 * LANES]
    hidden_grad = sums[:, 2 * LANES :]
    sig = jax.nn.sigmoid(gate_pre)
    hidden = (gate_pre * sig * up_pre).astype(bf16).astype(f32)
    route = jnp.sum(hidden * hidden_grad, axis=1, keepdims=True)
    scaled = weight * hidden_grad
    gate_grad = (scaled * up_pre * sig * (1.0 + gate_pre * (1.0 - sig))).astype(bf16)
    up_grad = (scaled * gate_pre * sig).astype(bf16)
    route_hi, route_lo = hi_lo(route)
    slots = route.shape[0]
    groups, tiles, toks, _ = back.shape
    lane = lax.broadcasted_iota(jnp.int32, (slots, LANES), 1)
    tags = jnp.where(lane == 0, route_hi, jnp.where(lane == 1, route_lo, 0.0))
    count = len(BLOCK_ORDER)
    tall = slots // count
    for index, slot in enumerate(BLOCK_ORDER):
        home = pl.multiple_of(lax.rem(place[0] + slot + count, count) * tall, tall)
        own = slice(index * tall, (index + 1) * tall)
        moved[pl.ds(home, tall), :LANES] = gate_grad[own]
        moved[pl.ds(home, tall), LANES : 2 * LANES] = up_grad[own]
        moved[pl.ds(home, tall), 2 * LANES :] = tags[own].astype(bf16)
    gate_grad, up_grad = moved[:, :LANES], moved[:, LANES : 2 * LANES]

    def put(k, tile):
        back[:, k] = tile.reshape(groups, toks, LANES).astype(bf16)

    put(tiles - 1, moved[:, 2 * LANES :].astype(f32))
    across = (((1,), (1,)), ((), ()))
    for k in range(0, tiles - 1, 2):
        cols = slice(k * LANES, (k + 2) * LANES)
        out = lax.dot_general(gate_grad, gate[cols], across, preferred_element_type=f32)
        out = out + lax.dot_general(up_grad, up[cols], across, preferred_element_type=f32)
        for j in range(2):
            put(k + j, out[:, j * LANES : (j + 1) * LANES])
    pairs = slots // 8
    weighted = (weight * hidden).reshape(pairs, 8, LANES)
    mask = upper(weighted.shape)
    even = jnp.where(mask, swap(weighted), 0.0)
    odd = jnp.where(mask, weighted, 0.0)
    wide[...] = jnp.stack([even, odd], axis=1).reshape(pairs * 16, LANES).astype(bf16)


def down_kernel(*refs):
    place = position()
    *found, wide, out, rows = refs
    blocks = [found[i] if j is None else found[i].at[j] for i, j in BLOCK_PICKS]
    lay_rows(place[2], blocks, BLOCK_OFFSETS, 0, rows)
    out[...] = lax.dot_general(
        wide[...], rows[...], (((0,), (0,)), ((), ())), preferred_element_type=jnp.float32
    ).astype(out.dtype)


def sum_kernel(sub, landed, pieces, acc):
    f32 = jnp.float32
    experts, owners, tiles, toks, _ = landed.shape
    tags = jnp.zeros((2 * toks, LANES), f32)
    lane = lax.broadcasted_iota(jnp.int32, (toks, LANES), 1)
    tag_hi = jnp.zeros((toks, LANES), f32)
    for e in range(experts):
        pair = landed[e, 0, tiles - 1].astype(f32)
        both = jnp.sum(jnp.where(lane < 2, pair, 0.0), axis=1, keepdims=True)
        tag_hi = jnp.where(lane == sub + e, both, tag_hi)
    tag_hi, tag_lo = hi_lo(tag_hi)
    acc[tiles - 1] = jnp.zeros_like(acc[tiles - 1])
    acc[tiles - 1, :toks] = tag_hi
    acc[tiles - 1, toks : 2 * toks] = tag_lo
    for k in range(tiles - 1):
        for q in range(owners):
            acc[k, q * toks : (q + 1) * toks] = jnp.sum(landed[:, q, k].astype(f32), axis=0)
    tags = acc[tiles - 1]
    lane = lax.broadcasted_iota(jnp.int32, tags.shape, 1)
    for m in range(pieces.shape[0]):
        first, skip = divmod(m * sub, LANES)
        tile = acc[first]
        if skip:
            tile = pltpu.roll(tile, LANES - skip, axis=1)
        if skip + sub > LANES:
            after = pltpu.roll(acc[first + 1], LANES - skip, axis=1)
            tile = jnp.where(lane < LANES - skip, tile, after)
        pieces[m] = jnp.where(lane < sub, tile, tags).astype(pieces.dtype)


def end_kernel(sub, final, ids, token_grad, route_grad, acc):
    f32 = jnp.float32
    toks, owners, _ = token_grad.shape
    acc[...] = jnp.sum(final[...].astype(f32), axis=0)
    for q in range(owners):
        token_grad[:, q, :] = acc[q * toks : (q + 1) * toks, :sub].astype(token_grad.dtype)
    routes = acc[:toks, :] + acc[toks : 2 * toks, :]
    lane = lax.broadcasted_iota(jnp.int32, routes.shape, 1) - sub
    cols = lax.broadcasted_iota(jnp.int32, ids.shape, 1)
    out = jnp.zeros(ids.shape, f32)
    for k in range(ids.shape[1]):
        hit = jnp.sum(jnp.where(lane == ids[:, k : k + 1], routes, 0.0), axis=1, keepdims=True)
        out = jnp.where(cols == k, hit, out)
    route_grad[...] = out


def weight_table(expert_ids, route_weights, experts):
    onehot = expert_ids[:, :, None] == jnp.arange(experts, dtype=jnp.int32)[None, None, :]
    weights = jnp.where(onehot, route_weights.astype(jnp.float32)[:, :, None], 0.0)
    return jnp.sum(weights, axis=1).astype(jnp.bfloat16)


def swap_with(block, toward):
    count = lax.axis_size("y")
    hops = []
    for y in range(count):
        for c in range(2):
            step = 1 if (y + c) % 2 == 0 else -1
            step = step if toward else -step
            hops.append((2 * y + c, 2 * ((y + step) % count) + c))
    return lax.ppermute(block, ("y", "c"), hops)


def body(tokens, out_grad, route_weights, expert_ids, w_gate, w_up, w_down):
    f32, bf16 = jnp.float32, jnp.bfloat16
    ny, nxh, nz = lax.axis_size("y"), lax.axis_size("xh"), lax.axis_size("z")
    experts = ny * nxh
    toks, _, sub = tokens.shape
    per_y = nxh * OWNERS
    groups = ny * per_y
    tall = 2 * toks
    table = weight_table(expert_ids, route_weights, experts)
    x_rows = jnp.concatenate(
        [tokens.transpose(1, 0, 2), jnp.broadcast_to(table[None], (OWNERS, toks, experts))], axis=2
    )
    g_rows = jnp.pad(out_grad.transpose(1, 0, 2), ((0, 0), (0, 0), (0, LANES - sub)))
    send = jnp.concatenate([x_rows, g_rows], axis=1)
    send = jnp.broadcast_to(send[None, :, None], (nxh, OWNERS, nz, tall, LANES))
    send = send.reshape(nxh * OWNERS * nz, tall, LANES)
    got = lax.all_to_all(send, ("xh", "xl", "c", "z"), 0, 0, tiled=True)
    tiles = nz * sub // LANES
    block = call(
        functools.partial(pack_kernel, sub),
        jax.ShapeDtypeStruct((tiles * per_y + 1, tall, LANES), bf16),
        whole(1),
        [],
        groups * tall * LANES,
        1 << 19,
    )(got.reshape(per_y, nz, tall, LANES))
    slots = groups * toks
    size = per_y * tall
    width = nz * sub

    def partial_sums(found, low, high, first):
        picks = BLOCK_PICKS[low:high]
        used = sorted({i for i, _ in picks})
        local = tuple((used.index(i), j) for i, j in picks)
        n = len(picks)
        part, weight = call(
            functools.partial(part_kernel, local, BLOCK_OFFSETS[low:high], first),
            (
                jax.ShapeDtypeStruct((n * per_y * toks, 3 * LANES), bf16),
                jax.ShapeDtypeStruct((n * per_y * toks, LANES), f32),
            ),
            whole(len(used) + 3),
            [pltpu.VMEM((n * size, width), bf16), pltpu.VMEM((n * size, LANES), f32)],
            PART_FLOPS,
            4 << 20,
        )(*[found[i] for i in used], w_gate[0], w_up[0], w_down[0])
        return lax.all_gather(part, ("xl", "c"), axis=0, tiled=False), weight

    first = swap_with(block, True)
    other = swap_with(block, False)
    beyond = swap_with(first, False)
    third = swap_with(jnp.stack([other, beyond]), True)
    found = [block, first, other, beyond, third]
    quad_a, weight_a = partial_sums(found, 0, 3, 0)
    third, quad_a = lax.optimization_barrier((third, quad_a))
    found[4] = third
    fourth = swap_with(third, False)
    quad_b, weight_b = partial_sums(found, 3, 5, 3)
    fourth, quad_b = lax.optimization_barrier((fourth, quad_b))
    found.append(fourth)
    quad_c, weight_c = partial_sums(found, 5, 8, 5)

    back, wide = call(
        grad_kernel,
        (
            jax.ShapeDtypeStruct((groups, tiles + 1, toks, LANES), bf16),
            jax.ShapeDtypeStruct((groups * tall, LANES), bf16),
        ),
        whole(8),
        [pltpu.VMEM((slots, 3 * LANES), bf16)],
        2 * slots * 2 * LANES * nz * LANES,
        3 << 20,
    )(quad_a, quad_b, quad_c, weight_a, weight_b, weight_c, w_gate[0], w_up[0])
    landed = lax.all_to_all(back, ("y", "xh", "xl", "c"), 0, 0, tiled=True)

    down_grad = call(
        down_kernel,
        jax.ShapeDtypeStruct((LANES, nz * sub), bf16),
        whole(len(found) + 1),
        [pltpu.VMEM((groups * tall, width), bf16)],
        2 * groups * tall * nz * LANES * LANES,
        4 << 20,
    )(*found, wide)
    pieces = call(
        functools.partial(sum_kernel, sub),
        jax.ShapeDtypeStruct((nz, OWNERS * toks, LANES), bf16),
        whole(1),
        [pltpu.VMEM((tiles + 1, OWNERS * toks, LANES), f32)],
        groups * toks * nz * LANES,
        1 << 20,
    )(landed.reshape(experts, OWNERS, tiles + 1, toks, LANES))
    final = lax.all_to_all(pieces, "z", 0, 0, tiled=True)
    token_grad, route_grad = call(
        functools.partial(end_kernel, sub),
        (
            jax.ShapeDtypeStruct((toks, OWNERS, sub), bf16),
            jax.ShapeDtypeStruct(expert_ids.shape, f32),
        ),
        whole(2),
        [pltpu.VMEM((OWNERS * toks, LANES), f32)],
        nz * OWNERS * toks * LANES,
        1 << 17,
    )(final, expert_ids)
    return token_grad, down_grad[None], route_grad


def solution(mesh):
    fine = Mesh(
        mesh.devices.reshape(-1, 2, 2, 2, mesh.devices.shape[1]), ("y", "xh", "xl", "c", "z")
    )
    group = ("y", "xh", "xl", "c")
    return jax.shard_map(
        body,
        mesh=fine,
        in_specs=(
            P(group, None, "z"),
            P(group, None, "z"),
            P(group, None),
            P(group, None),
            P(group, None, "z"),
            P(group, None, "z"),
            P(group, "z", None),
        ),
        out_specs=(P(group, None, "z"), P(group, "z", None), P(group, None)),
        check_vma=False,
    )
```
